512 devices in a mesh: ctx: 128 (over x, z, y_hi, core), ch: 4 (over y_lo).
Axes of the slice: x: 4, y: 8 (y_hi: 2, y_lo: 4; y = y_hi * 4 + y_lo), z: 8, core: 2. Of those that a mesh axis runs over, the one named last changes fastest.
Arguments:
- hyena_q: bfloat16 [16384, 4096], P('ctx', 'ch'), may hold values from -6 to 6
- hyena_k: bfloat16 [16384, 4096], P('ctx', 'ch'), may hold values from -6 to 6
- hyena_v: bfloat16 [16384, 4096], P('ctx', 'ch'), may hold values from -6 to 6
- short_taps: float32 [3, 3, 4096], P(None, None, 'ch'), may hold values from -3 to 3
- residues: float32 [16, 4096], P(None, 'ch'), may hold values from -1.5 to 1.5
- rates: float32 [16, 4096], P(None, 'ch'), may hold values from 6.1035157e-06 to 0.05
- queries: bfloat16 [16384, 4096], P('ctx', 'ch'), may hold values from -6 to 6
- keys: bfloat16 [16384, 4096], P('ctx', 'ch'), may hold values from -6 to 6
- offsets: int32 [128], replicated, may hold values from 0 to 24384, as said below
- block_mask: int32 [128, 6], P('ctx'), may hold values from 0 to 1, as said below
- out_gain: float32 [4096], P('ch'), may hold values from 0.5 to 1.5
Outputs:
- hyena_out: bfloat16 [16384, 4096], P('ctx', 'ch')
- attn_out: bfloat16 [16384, 4096], P('ctx', 'ch')
The draws below stay inside these ranges and needn't reach their ends.
Inputs may be any that keep to these rules, and one draw needn't show every extreme that they name: offsets[0] is 0, each offset exceeds the one before by 128 to 256, and the last offset is exactly (128 - 1) * 192. `block_mask`: columns 0 and 1 are 1 in every row.
All inputs are finite; a program needn't handle non-finite values.
Results may differ from the reference program's by a relative error of at most 0.029.
Values may be sent and summed in bfloat16 or wider, within the bound.
No kernel may reach another device: no remote copies, remote signals or barrier semaphores. Data moves between devices by JAX's collectives and lax.ppermute only.
A program may use at most 128 MiB of HBM per device.

```python
import math
import jax
import jax.numpy as jnp
from jax import lax

HEAD_DIM = 128
HEADS = 32
CH = 4096
MODES = 16
SUB = 32
STEPS = 6
TOK_DEV = 128
TOKENS = 16384
N_CTX = 128


def draw_offsets(key, part):
    half_gap = TOK_DEV // 2
    index_all = jnp.arange(N_CTX, dtype=jnp.int32)
    wobble = jax.random.randint(key, (N_CTX,), 0, half_gap + 1, dtype=jnp.int32)
    wobble = jnp.where((index_all == 0) | (index_all == N_CTX - 1), 0, wobble).astype(jnp.int32)
    following = jnp.concatenate([wobble[1:], jnp.zeros((1,), jnp.int32)])
    gaps = (half_gap + wobble - following).astype(jnp.int32)
    before = (jnp.cumsum(gaps) - gaps).astype(jnp.int32)
    return (index_all * TOK_DEV + before).astype(jnp.int32)


def draw_block_mask(key, part):
    bits = jax.random.randint(key, (N_CTX, STEPS), 0, 2, dtype=jnp.int32)
    column = jnp.arange(STEPS, dtype=jnp.int32)[None, :]
    return jnp.where(column <= 1, 1, bits).astype(jnp.int32)


def paired_fields(key):
    width = HEADS * HEAD_DIM
    query_out = jnp.clip(jax.random.normal(jax.random.fold_in(key, 11), (TOKENS, width), jnp.float32), -6.0, 6.0)
    key_out = jnp.clip(jax.random.normal(jax.random.fold_in(key, 12), (TOKENS, width), jnp.float32), -6.0, 6.0)
    return (query_out, key_out)


def draw_queries(key, part):
    return paired_fields(key)[0].astype(jnp.bfloat16)


def draw_keys(key, part):
    return paired_fields(key)[1].astype(jnp.bfloat16)


def level_of(key, dims, cuts, low, high):
    factor_of, own = 1.0, jax.random.fold_in(key, 6)
    for dim, parts in cuts:
        steps = jnp.exp(jax.random.uniform(jax.random.fold_in(own, dim), (parts,), jnp.float32, low / len(cuts), high / len(cuts)))
        factor_of = factor_of * jnp.repeat(steps, dims[dim] // parts).reshape([-1 if axis == dim else 1 for axis in range(len(dims))])
    return factor_of


def bell_draw(stream_key, dims, spread, limit, cuts=(), kind=jnp.bfloat16):
    array = spread * jax.random.normal(stream_key, dims, jnp.float32)
    if cuts:
        array = array * level_of(stream_key, dims, cuts, -0.22, 0.18)
    return jnp.clip(array, -limit, limit).astype(kind)


def setup_inputs(seed: int = 0) -> dict:
    seeds = jax.random.split(jax.random.key(seed), 12)
    return {
        "hyena_q": bell_draw(seeds[0], (TOKENS, CH), 1.0, 6.0, ((0, 128), (1, 4))),
        "hyena_k": bell_draw(seeds[1], (TOKENS, CH), 1.0, 6.0, ((0, 128), (1, 4))),
        "hyena_v": bell_draw(seeds[2], (TOKENS, CH), 1.0, 6.0, ((0, 128), (1, 4))),
        "short_taps": bell_draw(seeds[3], (3, 3, CH), 0.6, 3.0, ((2, 4),), jnp.float32),
        "residues": bell_draw(seeds[4], (MODES, CH), MODES ** -0.5, 1.5, ((1, 4),), jnp.float32),
        "rates": jnp.clip(jnp.exp(math.log(0.05) - 9.010913 * jax.random.uniform(seeds[5], (MODES, CH), jnp.float32) ** level_of(seeds[5], (MODES, CH), ((1, 4),), -0.2, 0.2)), 6.10351571594947e-06, 0.05),
        "queries": draw_queries(jax.random.fold_in(seeds[11], 71), 0),
        "keys": draw_keys(jax.random.fold_in(seeds[11], 71), 0),
        "offsets": draw_offsets(jax.random.fold_in(seeds[11], 71), 0),
        "block_mask": draw_block_mask(jax.random.fold_in(seeds[11], 71), 0),
        "out_gain": jnp.clip(1.0 + 0.1 * jax.random.normal(seeds[10], (HEADS * HEAD_DIM,), jnp.float32), 0.5, 1.5),
    }


orig_window = 8192.0
rope_base = 10000.0
yarn_factor = 128.0
norm_eps = 1e-05
highest = lax.Precision.HIGHEST

def head_freqs(head_dim):
    half_dim = head_dim // 2
    base_freq = jnp.power(rope_base, -2.0 * jnp.arange(half_dim, dtype=jnp.float32) / head_dim)
    wave_ratio = orig_window * base_freq / (2.0 * math.pi)
    ramp_mix = jnp.clip((wave_ratio - 1.0) / 31.0, 0.0, 1.0)
    freq_table = base_freq * ramp_mix + base_freq / yarn_factor * (1.0 - ramp_mix)
    yarn_scale = 0.1 * math.log(yarn_factor) + 1.0
    return (freq_table, yarn_scale)

def rotate(x, positions, freq_table):
    half_dim = x.shape[2] // 2
    angles = positions.astype(jnp.float32)[:, None, None] * freq_table[None, None, :]
    cosine = jnp.cos(angles)
    sine = jnp.sin(angles)
    lead_half = x[:, :, :half_dim]
    tail_half = x[:, :, half_dim:]
    return jnp.concatenate([lead_half * cosine - tail_half * sine, tail_half * cosine + lead_half * sine], axis=2)

def round_trip(x):
    return lax.optimization_barrier(x.astype(jnp.bfloat16)).astype(jnp.float32)

def featurize(x, tap_set):
    x_float = x.astype(jnp.float32)
    padded = jnp.pad(x_float, ((2, 0), (0, 0)))
    count = x.shape[0]
    return tap_set[0] * padded[2:] + tap_set[1] * padded[1:count + 1] + tap_set[2] * padded[:count]

def modal_tables(residues, rates, sub):
    gain_mode = residues * jnp.sqrt(-jnp.expm1(-2.0 * rates))
    step_idx = jnp.arange(sub, dtype=jnp.int32)
    lag_value = step_idx.astype(jnp.float32)
    filter_sub = jnp.einsum('mc,mnc->nc', gain_mode, jnp.exp(-rates[:, None, :] * lag_value[None, :, None]), precision=highest)
    lag_index = step_idx[:, None] - step_idx[None, :]
    one_hot = (lag_index[:, :, None] == step_idx[None, None, :]).astype(jnp.float32)
    toeplitz = jnp.einsum('tsn,nc->tsc', one_hot, filter_sub, precision=highest)
    end_decay = jnp.exp(-rates[:, None, :] * (sub - 1.0 - lag_value)[None, :, None])
    read_decay = gain_mode[:, None, :] * jnp.exp(-rates[:, None, :] * (lag_value + 1.0)[None, :, None])
    return (toeplitz, end_decay, read_decay)

def stretch_local(mixed, toeplitz, end_decay, rates, sub):
    tok_rows, chan_count = mixed.shape
    sub_count = tok_rows // sub
    blocks = mixed.reshape(sub_count, sub, chan_count)
    near_part = jnp.einsum('tsc,bsc->btc', toeplitz, blocks, precision=highest).reshape(tok_rows, chan_count)
    inflow = jnp.einsum('msc,bsc->bmc', end_decay, blocks, precision=highest)
    step_decay = jnp.exp(-rates * sub)

    def advance(state_now, block_in):
        return (step_decay * state_now + block_in, state_now)
    final_state, start_state = lax.scan(advance, jnp.zeros_like(rates), inflow)
    return (near_part, start_state, final_state)

def stretch_far(read_decay, start_state, carry_in, rates, sub):
    sub_count = start_state.shape[0]
    lead_span = (sub * jnp.arange(sub_count, dtype=jnp.int32)).astype(jnp.float32)
    lead_decay = jnp.exp(-rates[None, :, :] * lead_span[:, None, None])
    full_state = start_state + lead_decay * carry_in[None, :, :]
    far_part = jnp.einsum('mtc,bmc->btc', read_decay, full_state, precision=highest)
    return far_part.reshape(sub_count * sub, rates.shape[1])

def reference(hyena_q, hyena_k, hyena_v, short_taps, residues, rates, queries, keys, offsets, block_mask, out_gain):
    feat_q = featurize(hyena_q, short_taps[0])
    feat_k = featurize(hyena_k, short_taps[1])
    feat_v = featurize(hyena_v, short_taps[2])
    mixed = feat_k * feat_v
    toeplitz, end_decay, read_decay = modal_tables(residues, rates, SUB)
    stretch_decay = jnp.exp(-rates * TOK_DEV)

    def advance_stretch(carry_in, mixed_stretch):
        near_part, start_state, final_state = stretch_local(mixed_stretch, toeplitz, end_decay, rates, SUB)
        far_part = stretch_far(read_decay, start_state, carry_in, rates, SUB)
        return (stretch_decay * carry_in + final_state, near_part + far_part)
    last_state, long_conv = lax.scan(advance_stretch, jnp.zeros_like(rates), mixed.reshape(N_CTX, TOK_DEV, CH))
    hyena_out = (feat_q * long_conv.reshape(TOKENS, CH)).astype(jnp.bfloat16)
    freq_table, yarn_scale = head_freqs(HEAD_DIM)
    score_coef = yarn_scale * yarn_scale / math.sqrt(HEAD_DIM)
    q_stretches = queries.reshape(N_CTX, TOK_DEV, HEADS, HEAD_DIM)
    k_stretches = keys.reshape(N_CTX, TOK_DEV, HEADS, HEAD_DIM)
    v_stretches = hyena_out.reshape(N_CTX, TOK_DEV, HEADS, HEAD_DIM)
    position = jnp.arange(TOK_DEV, dtype=jnp.int32)

    def attend(stretch_index):
        query_pos = offsets[stretch_index] + position
        q_rot = round_trip(rotate(q_stretches[stretch_index].astype(jnp.float32), query_pos, freq_table))
        key_list, value_list, vis_list = ([], [], [])
        for step_back in range(STEPS):
            source = (stretch_index - step_back) % N_CTX
            key_pos = offsets[source] + position
            key_list.append(round_trip(rotate(k_stretches[source].astype(jnp.float32), key_pos, freq_table)))
            value_list.append(v_stretches[source].astype(jnp.float32))
            allowed = block_mask[stretch_index, step_back] == 1
            if step_back == 0:
                vis_list.append((key_pos[None, :] <= query_pos[:, None]) & allowed)
            else:
                vis_list.append(jnp.broadcast_to(allowed, (TOK_DEV, TOK_DEV)))
        key_all = jnp.concatenate(key_list, axis=0)
        value_all = jnp.concatenate(value_list, axis=0)
        visible = jnp.concatenate(vis_list, axis=1)
        scores = jnp.einsum('qhd,khd->hqk', q_rot, key_all, precision=highest) * score_coef
        masked = jnp.where(visible[None], scores, -1e+30)
        row_max = lax.optimization_barrier(jnp.max(masked, axis=2, keepdims=True))
        weights = jnp.where(visible[None], jnp.exp(masked - row_max), 0.0)
        row_sum = lax.optimization_barrier(jnp.sum(weights, axis=2))
        attended = jnp.einsum('hqk,khd->qhd', round_trip(weights), value_all, precision=highest)
        return attended / jnp.transpose(row_sum)[:, :, None]
    attended = lax.map(attend, jnp.arange(N_CTX, dtype=jnp.int32)).reshape(TOKENS, HEADS * HEAD_DIM)
    mean_sq = lax.optimization_barrier(jnp.mean(attended * attended, axis=1))
    attn_out = (attended * lax.rsqrt(mean_sq + norm_eps)[:, None] * out_gain[None, :]).astype(jnp.bfloat16)
    return (hyena_out, attn_out)
```

```python
import math

import jax
import jax.numpy as jnp
from jax import lax
from jax.experimental import pallas as pl
from jax.experimental.pallas import tpu as pltpu
from jax.sharding import PartitionSpec as P

HEAD_DIM = 128
MODES = 16
TOK = 128
WIDTH = 1024
HEADS = WIDTH // HEAD_DIM
LANES = 128
ROWS = WIDTH // LANES
NX, NZ, NQ = 4, 8, 4
N_CTX = NX * NZ * NQ

orig_window = 8192.0
rope_base = 10000.0
yarn_factor = 128.0
norm_eps = 1e-05
f32 = jnp.float32
bf16 = jnp.bfloat16


def call(kernel, out_shape, args, scratch=(), smem=(), flops=1000000):
    specs = [
        pl.BlockSpec(memory_space=pltpu.SMEM if i in smem else pltpu.VMEM)
        for i in range(len(args))
    ]
    single = not isinstance(out_shape, (list, tuple))
    outs = pl.BlockSpec(memory_space=pltpu.VMEM)
    return pl.pallas_call(
        kernel,
        out_shape=out_shape,
        in_specs=specs,
        out_specs=outs if single else [outs] * len(out_shape),
        scratch_shapes=list(scratch),
        compiler_params=pltpu.CompilerParams(vmem_limit_bytes=24 * 1024 * 1024),
        cost_estimate=pl.CostEstimate(flops=flops, bytes_accessed=1000000, transcendentals=0),
    )(*args)


def sds(shape, dtype):
    return jax.ShapeDtypeStruct(shape, dtype)


def head_freqs(head_dim):
    half_dim = head_dim // 2
    base_freq = jnp.power(rope_base, -2.0 * jnp.arange(half_dim, dtype=f32) / head_dim)
    wave_ratio = orig_window * base_freq / (2.0 * math.pi)
    ramp_mix = jnp.clip((wave_ratio - 1.0) / 31.0, 0.0, 1.0)
    return base_freq * ramp_mix + base_freq / yarn_factor * (1.0 - ramp_mix)


def lane_block(j):
    return slice(j * LANES, (j + 1) * LANES)


def tok_rows(t):
    return pl.ds(pl.multiple_of(t * ROWS, ROWS), ROWS)


def tree_sum(items):
    items = list(items)
    while len(items) > 1:
        items = [
            items[i] + items[i + 1] if i + 1 < len(items) else items[i]
            for i in range(0, len(items), 2)
        ]
    return items[0]


def modes_of(ref):
    return [ref[m * ROWS : (m + 1) * ROWS, :] for m in range(MODES)]


def rotate_kernel(q_ref, k_ref, cos_ref, sin_ref, qo_ref, ko_ref):
    cosine = cos_ref[...]
    sine = sin_ref[...]
    for src, dst in ((k_ref, ko_ref), (q_ref, qo_ref)):
        for h in range(HEADS):
            x = src[:, lane_block(h)].astype(f32)
            dst[:, lane_block(h)] = (x * cosine + pltpu.roll(x, HEAD_DIM // 2, 1) * sine).astype(bf16)


def local_kernel(
    q_ref, k_ref, v_ref, taps_ref, res_ref, rate_ref,
    l_ref, fq_ref, f0_ref, rr_ref, gg_ref, tp_ref, edge_ref,
    qs, ks, vs, rs,
):
    for part in range(MODES // 8):
        for j in range(ROWS):
            rows = pl.ds(part * 8 * ROWS + j, 8, stride=ROWS)
            rr_ref[rows, :] = rate_ref[part * 8 : part * 8 + 8, lane_block(j)]
            rs[rows, :] = res_ref[part * 8 : part * 8 + 8, lane_block(j)]
    for a in range(3):
        for j in range(ROWS):
            tp_ref[pl.ds(a * 3 * ROWS + j, 3, stride=ROWS), :] = taps_ref[a, :, lane_block(j)]
    for src, dst in ((k_ref, ks), (v_ref, vs), (q_ref, qs)):
        for g in range(TOK // 16):
            block = src[g * 16 : (g + 1) * 16, :].astype(f32)
            for s in range(2):
                for j in range(ROWS):
                    dst[pl.ds((g * 16 + s * 8) * ROWS + j, 8, stride=ROWS), :] = block[
                        s * 8 : s * 8 + 8, lane_block(j)
                    ]
    for i, src in enumerate((ks, vs, qs)):
        edge_ref[i * 2 * ROWS : (i + 1) * 2 * ROWS, :] = src[0 : 2 * ROWS, :]
    rate = rr_ref[...]
    x = 2.0 * rate
    series = x * (1.0 - x / 2.0 * (1.0 - x / 3.0 * (1.0 - x / 4.0 * (
        1.0 - x / 5.0 * (1.0 - x / 6.0 * (1.0 - x / 7.0))))))
    gg_ref[...] = rs[...] * jnp.sqrt(series)
    rs[...] = jnp.exp(-rate)
    decay = modes_of(rs)
    gain = modes_of(gg_ref)
    tap = [tp_ref[i * ROWS : (i + 1) * ROWS, :] for i in range(9)]
    unroll = 6

    def step(it, carry):
        state = list(carry)
        for o in range(unroll):
            t = it * unroll + 2 + o
            now, one, two = tok_rows(t), tok_rows(t - 1), tok_rows(t - 2)
            feat_k = tap[3] * ks[now, :] + tap[4] * ks[one, :] + tap[5] * ks[two, :]
            feat_v = tap[6] * vs[now, :] + tap[7] * vs[one, :] + tap[8] * vs[two, :]
            fq_ref[now, :] = tap[0] * qs[now, :] + tap[1] * qs[one, :] + tap[2] * qs[two, :]
            mixed = feat_k * feat_v
            state = [decay[m] * state[m] + gain[m] * mixed for m in range(MODES)]
            l_ref[now, :] = tree_sum(state)
        return tuple(state)

    zero = jnp.zeros((ROWS, LANES), f32)
    state = lax.fori_loop(0, (TOK - 2) // unroll, step, (zero,) * MODES)
    for m in range(MODES):
        f0_ref[m * ROWS : (m + 1) * ROWS, :] = state[m]


def edge_kernel(halo_ref, edge_ref, tp_ref, rr_ref, gg_ref, f0_ref, f_ref, em_ref, hs):
    halo = halo_ref[...].astype(f32)
    for j in range(ROWS):
        hs[pl.ds(j, 8, stride=ROWS), :] = halo[:, lane_block(j)]

    def row(ref, i):
        return ref[i * ROWS : (i + 1) * ROWS, :]

    tap = [row(tp_ref, i) for i in range(9)]

    def feats(i, base):
        prev2, prev1 = row(hs, 2 * i), row(hs, 2 * i + 1)
        tok0, tok1 = row(edge_ref, 2 * i), row(edge_ref, 2 * i + 1)
        w = tap[base : base + 3]
        return (
            w[0] * tok0 + w[1] * prev1 + w[2] * prev2,
            w[0] * tok1 + w[1] * tok0 + w[2] * prev1,
        )

    k0, k1 = feats(0, 3)
    v0, v1 = feats(1, 6)
    q0, q1 = feats(2, 0)
    m0, m1 = k0 * v0, k1 * v1
    for i, value in enumerate((m0, m1, q0, q1)):
        em_ref[i * ROWS : (i + 1) * ROWS, :] = value
    for i in range(MODES // 2):
        both = []
        for m in (2 * i, 2 * i + 1):
            rate, gain = row(rr_ref, m), row(gg_ref, m)
            both.append(
                row(f0_ref, m)
                + gain * (jnp.exp(rate * -127.0) * m0 + jnp.exp(rate * -126.0) * m1)
            )
        f_ref[i * 2 * ROWS : (i + 1) * 2 * ROWS, :] = jnp.concatenate(both, axis=0).astype(bf16)


def weight(rate, span, steps):
    factor = jnp.exp(rate * (jnp.maximum(steps, 0) * -span).astype(f32))
    return jnp.where(steps >= 0, factor, 0.0)


def quad_kernel(idx_ref, fq_ref, rr_ref, t_ref, before_ref):
    q = idx_ref[2]
    rate = rr_ref[...]
    f = [fq_ref[i * LANES : (i + 1) * LANES, :].astype(f32) for i in range(NQ)]
    d1 = jnp.exp(rate * -float(TOK))
    total = f[0]
    for i in range(1, NQ):
        total = d1 * total + f[i]
    total = total.astype(bf16)
    for i in range(NZ):
        t_ref[i] = total
    before_ref[...] = tree_sum([weight(rate, TOK, q - 1 - i) * f[i] for i in range(NQ - 1)])


def z_kernel(idx_ref, tz_ref, rr_ref, u_ref, before_ref):
    z = idx_ref[1]
    rate = rr_ref[...]
    d = jnp.exp(rate * -float(TOK * NQ))
    total = tz_ref[0].astype(f32)
    before = jnp.zeros_like(total)
    for i in range(1, NZ):
        before = jnp.where(z == i, total, before)
        total = d * total + tz_ref[i].astype(f32)
    total = total.astype(bf16)
    for i in range(NX):
        u_ref[i] = total
    before_ref[...] = before


def out_kernel(idx_ref, ux_ref, zb_ref, qb_ref, rr_ref, gg_ref, em_ref, l_ref, fq_ref, out_ref, cs, ys):
    x, z, q = idx_ref[0], idx_ref[1], idx_ref[2]
    rate = rr_ref[...]
    d = jnp.exp(rate * -float(TOK * NQ * NZ))
    carry = jnp.zeros_like(rate)
    running = ux_ref[0].astype(f32)
    for i in range(1, NX):
        carry = jnp.where(x == i, running, carry)
        if i < NX - 1:
            running = d * running + ux_ref[i].astype(f32)
    group = zb_ref[...] + jnp.exp(rate * (z * -(TOK * NQ)).astype(f32)) * carry
    own = qb_ref[...] + jnp.exp(rate * (q * -TOK).astype(f32)) * group
    decay_all = jnp.exp(-rate)
    gain_all = gg_ref[...]

    def tile(value, m):
        return value[m * ROWS : (m + 1) * ROWS, :]

    decay = [tile(decay_all, m) for m in range(MODES)]
    m0, m1, q0, q1 = [em_ref[i * ROWS : (i + 1) * ROWS, :] for i in range(4)]
    state = [decay[m] * tile(own, m) + tile(gain_all, m) * m0 for m in range(MODES)]
    ys[0:ROWS, :] = q0 * tree_sum(state)
    state = [decay[m] * state[m] + tile(gain_all, m) * m1 for m in range(MODES)]
    ys[ROWS : 2 * ROWS, :] = q1 * tree_sum(state)
    for m in range(MODES):
        cs[m * ROWS : (m + 1) * ROWS, :] = tile(decay_all, m)
    unroll = 6

    def step(it, carry_now):
        state = list(carry_now)
        for o in range(unroll):
            now = tok_rows(it * unroll + 2 + o)
            state = [cs[m * ROWS : (m + 1) * ROWS, :] * state[m] for m in range(MODES)]
            ys[now, :] = fq_ref[now, :] * (l_ref[now, :] + tree_sum(state))
        return tuple(state)

    lax.fori_loop(0, (TOK - 2) // unroll, step, tuple(state))
    for g in range(TOK // 16):
        for j in range(ROWS):
            halves = [
                ys[pl.ds((g * 16 + s * 8) * ROWS + j, 8, stride=ROWS), :] for s in range(2)
            ]
            out_ref[g * 16 : (g + 1) * 16, lane_block(j)] = jnp.concatenate(halves, axis=0).astype(bf16)


def weights_kernel(mask_ref, q_ref, k0_ref, k1_ref, k2_ref, k3_ref, k4_ref, k5_ref, w_ref, inv_ref):
    yarn_scale = 0.1 * math.log(yarn_factor) + 1.0
    coef = yarn_scale * yarn_scale / math.sqrt(HEAD_DIM) * math.log2(math.e)
    pieces = (k0_ref, k1_ref, k2_ref, k3_ref, k4_ref, k5_ref)
    shape = (TOK, TOK)
    causal = lax.broadcasted_iota(jnp.int32, shape, 1) <= lax.broadcasted_iota(jnp.int32, shape, 0)
    lane = lax.broadcasted_iota(jnp.int32, (TOK, LANES), 1)
    inverse = jnp.zeros((TOK, LANES), f32)
    for h in range(HEADS):
        query = q_ref[:, lane_block(h)]
        scores = []
        for i, piece in enumerate(pieces):
            s = lax.dot_general(
                query, piece[:, lane_block(h)], (((1,), (1,)), ((), ())), preferred_element_type=f32
            ) * coef
            allowed = mask_ref[i] == 1
            visible = (causal & allowed) if i == 0 else jnp.broadcast_to(allowed, shape)
            scores.append(jnp.where(visible, s, -1e30))
        top = scores[0]
        for s in scores[1:]:
            top = jnp.maximum(top, s)
        top = jnp.max(top, axis=1, keepdims=True)
        total = None
        for i, s in enumerate(scores):
            w = jnp.exp2(s - top)
            total = w if total is None else total + w
            w_ref[h, :, lane_block(i)] = w.astype(bf16)
        total = jnp.sum(total, axis=1, keepdims=True)
        inverse = jnp.where(lane == h, 1.0 / total, inverse)
    inv_ref[...] = inverse


def attend_kernel(w_ref, inv_ref, v0_ref, v1_ref, v2_ref, v3_ref, v4_ref, v5_ref, a_ref, sq_ref):
    pieces = (v0_ref, v1_ref, v2_ref, v3_ref, v4_ref, v5_ref)
    inverse = inv_ref[...]
    squares = None
    for h in range(HEADS):
        acc = None
        for i, piece in enumerate(pieces):
            part = jnp.dot(w_ref[h, :, lane_block(i)], piece[:, lane_block(h)], preferred_element_type=f32)
            acc = part if acc is None else acc + part
        acc = acc * inverse[:, h : h + 1]
        a_ref[:, lane_block(h)] = acc
        squares = acc * acc if squares is None else squares + acc * acc
    sums = jnp.sum(squares, axis=1, keepdims=True)
    shape = (TOK, TOK)
    diag = lax.broadcasted_iota(jnp.int32, shape, 1) == lax.broadcasted_iota(jnp.int32, shape, 0)
    sq_ref[...] = jnp.sum(jnp.where(diag, sums, 0.0), axis=0, keepdims=True)


def norm_kernel(a_ref, sq_ref, gain_ref, out_ref):
    shape = (TOK, TOK)
    diag = lax.broadcasted_iota(jnp.int32, shape, 1) == lax.broadcasted_iota(jnp.int32, shape, 0)
    sums = jnp.sum(jnp.where(diag, sq_ref[...], 0.0), axis=1, keepdims=True)
    scale = lax.rsqrt(sums / float(WIDTH * 4) + norm_eps)
    out_ref[...] = (a_ref[...] * scale * gain_ref[...]).astype(bf16)


def quad_groups():
    return [[g * NQ + q for q in range(NQ)] for g in range(NX * NZ)]


def z_groups():
    return [[(x * NZ + z) * NQ + q for z in range(NZ)] for x in range(NX) for q in range(NQ)]


def x_groups():
    return [[(x * NZ + z) * NQ + q for x in range(NX)] for z in range(NZ) for q in range(NQ)]


def ahead(value, steps):
    return lax.ppermute(value, "ctx", [(i, (i + steps) % N_CTX) for i in range(N_CTX)])


def core_swap(value):
    return lax.ppermute(value, "ctx", [(i, i ^ 1) for i in range(N_CTX)])


def window(value):
    extra = lax.ppermute(
        value, "ctx", [(i, (i + (5 if i % 2 else 1)) % N_CTX) for i in range(N_CTX)]
    )
    two = ahead(value, 2)
    four = ahead(value, 4)
    return [value, two, four, core_swap(two), core_swap(four), extra]


def local(
    hyena_q, hyena_k, hyena_v, short_taps, residues, rates, queries, keys, offsets, block_mask, out_gain
):
    me = lax.axis_index("ctx")
    idx = jnp.stack([me // (NZ * NQ), (me // NQ) % NZ, me % NQ]).astype(jnp.int32)
    rim = jnp.concatenate(
        [hyena_k[TOK - 2 :], hyena_v[TOK - 2 :], hyena_q[TOK - 2 :], hyena_q[TOK - 2 :]], axis=0
    )
    halo = lax.ppermute(rim, "ctx", [(i, i + 1) for i in range(N_CTX - 1)])

    angles = (offsets[me] + jnp.arange(TOK, dtype=jnp.int32)).astype(f32)[:, None] * head_freqs(HEAD_DIM)[None, :]
    cosine, sine = jnp.cos(angles), jnp.sin(angles)
    q_rot, k_rot = call(
        rotate_kernel,
        [sds((TOK, WIDTH), bf16)] * 2,
        (
            queries,
            keys,
            jnp.concatenate([cosine, cosine], axis=1),
            jnp.concatenate([-sine, sine], axis=1),
        ),
    )
    key_pieces = window(k_rot)

    big, small = sds((TOK * ROWS, LANES), f32), sds((MODES * ROWS, LANES), f32)
    l_rest, feat_q, f0, rr, gg, tp, edge = call(
        local_kernel,
        [big, big, small, small, small, sds((9 * ROWS, LANES), f32), sds((6 * ROWS, LANES), f32)],
        (hyena_q, hyena_k, hyena_v, short_taps, residues, rates),
        scratch=[pltpu.VMEM((TOK * ROWS, LANES), f32)] * 3 + [pltpu.VMEM((MODES * ROWS, LANES), f32)],
    )
    state, em = call(
        edge_kernel,
        [sds((MODES * ROWS, LANES), bf16), sds((4 * ROWS, LANES), f32)],
        (halo, edge, tp, rr, gg, f0),
        scratch=[pltpu.VMEM((8 * ROWS, LANES), f32)],
    )
    quad = lax.all_gather(state, "ctx", axis_index_groups=quad_groups(), tiled=True)
    group, quad_before = call(
        quad_kernel, [sds((NZ, MODES * ROWS, LANES), bf16), small], (idx, quad, rr), smem=(0,)
    )
    along_z = lax.all_to_all(group, "ctx", 0, 0, tiled=True, axis_index_groups=z_groups())
    column, z_before = call(
        z_kernel, [sds((NX, MODES * ROWS, LANES), bf16), small], (idx, along_z, rr), smem=(0,)
    )
    along_x = lax.all_to_all(column, "ctx", 0, 0, tiled=True, axis_index_groups=x_groups())
    hyena_out = call(
        out_kernel,
        sds((TOK, WIDTH), bf16),
        (idx, along_x, z_before, quad_before, rr, gg, em, l_rest, feat_q),
        scratch=[pltpu.VMEM((MODES * ROWS, LANES), f32), pltpu.VMEM((TOK * ROWS, LANES), f32)],
        smem=(0,),
    )
    value_pieces = window(hyena_out)

    order = jnp.where(
        me % 2 == 0, jnp.array([0, 2, 4, 1, 3, 5], jnp.int32), jnp.array([0, 2, 4, 3, 5, 1], jnp.int32)
    )
    weights, inverse = call(
        weights_kernel,
        [sds((HEADS, TOK, 6 * TOK), bf16), sds((TOK, LANES), f32)],
        (block_mask[0][order], q_rot, *key_pieces),
        smem=(0,),
    )
    attended, squares = call(
        attend_kernel,
        [sds((TOK, WIDTH), f32), sds((1, TOK), f32)],
        (weights, inverse, *value_pieces),
    )
    total = lax.psum(squares, "ch")
    attn_out = call(norm_kernel, sds((TOK, WIDTH), bf16), (attended, total, out_gain[None, :]))
    return (hyena_out, attn_out)


def solution(mesh):
    return jax.shard_map(
        local,
        mesh=mesh,
        in_specs=(
            P("ctx", "ch"),
            P("ctx", "ch"),
            P("ctx", "ch"),
            P(None, None, "ch"),
            P(None, "ch"),
            P(None, "ch"),
            P("ctx", "ch"),
            P("ctx", "ch"),
            P(),
            P("ctx", None),
            P("ch"),
        ),
        out_specs=(P("ctx", "ch"), P("ctx", "ch")),
        check_vma=False,
    )
```

```python
import math

import jax
import jax.numpy as jnp
from jax import lax
from jax.experimental import pallas as pl
from jax.experimental.pallas import tpu as pltpu
from jax.sharding import PartitionSpec as P

HEAD_DIM = 128
MODES = 16
TOK = 128
WIDTH = 1024
HEADS = WIDTH // HEAD_DIM
LANES = 128
ROWS = WIDTH // LANES
NX, NZ, NQ = 4, 8, 4
N_CTX = NX * NZ * NQ
EVEN_STEPS = (0, 2, 4, 1, 3, 5)
ODD_STEPS = (0, 2, 4, 3, 5, 1)

orig_window = 8192.0
rope_base = 10000.0
yarn_factor = 128.0
norm_eps = 1e-05
f32 = jnp.float32
bf16 = jnp.bfloat16


def call(kernel, out_shape, args, scratch=(), smem=(), hbm=(), vmem=24, flops=1000000):
    specs = [
        pl.BlockSpec(
            memory_space=pltpu.SMEM if i in smem else pltpu.HBM if i in hbm else pltpu.VMEM
        )
        for i in range(len(args))
    ]
    single = not isinstance(out_shape, (list, tuple))
    outs = pl.BlockSpec(memory_space=pltpu.VMEM)
    return pl.pallas_call(
        kernel,
        out_shape=out_shape,
        in_specs=specs,
        out_specs=outs if single else [outs] * len(out_shape),
        scratch_shapes=list(scratch),
        compiler_params=pltpu.CompilerParams(vmem_limit_bytes=vmem * 1024 * 1024),
        cost_estimate=pl.CostEstimate(flops=flops, bytes_accessed=1000000, transcendentals=0),
    )(*args)


def sds(shape, dtype):
    return jax.ShapeDtypeStruct(shape, dtype)


def head_freqs(head_dim):
    half_dim = head_dim // 2
    base_freq = jnp.power(rope_base, -2.0 * jnp.arange(half_dim, dtype=f32) / head_dim)
    wave_ratio = orig_window * base_freq / (2.0 * math.pi)
    ramp_mix = jnp.clip((wave_ratio - 1.0) / 31.0, 0.0, 1.0)
    return base_freq * ramp_mix + base_freq / yarn_factor * (1.0 - ramp_mix)


def lane_block(j):
    return slice(j * LANES, (j + 1) * LANES)


def tok_rows(t):
    return pl.ds(pl.multiple_of(t * ROWS, ROWS), ROWS)


def tree_sum(items):
    items = list(items)
    while len(items) > 1:
        items = [
            items[i] + items[i + 1] if i + 1 < len(items) else items[i]
            for i in range(0, len(items), 2)
        ]
    return items[0]


def modes_of(ref):
    return [ref[m * ROWS : (m + 1) * ROWS, :] for m in range(MODES)]


def fetch(pairs, sems):
    copies = [
        pltpu.make_async_copy(src, dst, sems.at[i]) for i, (src, dst) in enumerate(pairs)
    ]
    for copy in copies:
        copy.start()
    return copies


def rotate_kernel(q_hbm, k_hbm, cos_ref, sin_ref, qo_ref, ko_ref, q_ref, k_ref, sems):
    for copy in fetch([(q_hbm, q_ref), (k_hbm, k_ref)], sems):
        copy.wait()
    cosine = cos_ref[...]
    sine = sin_ref[...]
    for src, dst in ((k_ref, ko_ref), (q_ref, qo_ref)):
        for h in range(HEADS):
            x = src[:, lane_block(h)].astype(f32)
            dst[:, lane_block(h)] = (x * cosine + pltpu.roll(x, HEAD_DIM // 2, 1) * sine).astype(bf16)


T_STATE, T_RATE, T_GAIN, T_TAP, T_EDGE, T_END = 0, 128, 256, 384, 456, 504


def copy_kernel(src_ref, dst_ref):
    dst_ref[...] = src_ref[...]


def pair_kernel(a_ref, b_ref, out_ref):
    out_ref[0] = a_ref[...]
    out_ref[1] = b_ref[...]


def local_kernel(h_ref, p_ref, l_ref, fq_ref, table_ref, qs, ks, vs, rs):
    f0_ref = table_ref.at[T_STATE:T_RATE]
    rr_ref = table_ref.at[T_RATE:T_GAIN]
    gg_ref = table_ref.at[T_GAIN:T_TAP]
    tp_ref = table_ref.at[T_TAP:T_EDGE]
    edge_ref = table_ref.at[T_EDGE:T_END]
    for part in range(MODES // 8):
        for j in range(ROWS):
            rows = pl.ds(part * 8 * ROWS + j, 8, stride=ROWS)
            rr_ref[rows, :] = p_ref[part * 8 : part * 8 + 8, lane_block(j)]
            rs[rows, :] = p_ref[MODES + part * 8 : MODES + part * 8 + 8, lane_block(j)]
    for j in range(ROWS):
        tp_ref[pl.ds(j, 8, stride=ROWS), :] = p_ref[2 * MODES : 2 * MODES + 8, lane_block(j)]
        tp_ref[8 * ROWS + j : 8 * ROWS + j + 1, :] = p_ref[2 * MODES + 8 : 2 * MODES + 9, lane_block(j)]
    for i, dst in enumerate((ks, vs, qs)):
        for g in range(TOK // 16):
            block = h_ref[i * TOK + g * 16 : i * TOK + (g + 1) * 16, :].astype(f32)
            for s in range(2):
                for j in range(ROWS):
                    dst[pl.ds((g * 16 + s * 8) * ROWS + j, 8, stride=ROWS), :] = block[
                        s * 8 : s * 8 + 8, lane_block(j)
                    ]
    for i, src in enumerate((ks, vs, qs)):
        edge_ref[i * 2 * ROWS : (i + 1) * 2 * ROWS, :] = src[0 : 2 * ROWS, :]
    rate = rr_ref[...]
    x = 2.0 * rate
    series = x * (1.0 - x / 2.0 * (1.0 - x / 3.0 * (1.0 - x / 4.0 * (
        1.0 - x / 5.0 * (1.0 - x / 6.0 * (1.0 - x / 7.0))))))
    gg_ref[...] = rs[...] * jnp.sqrt(series)
    rs[...] = jnp.exp(-rate)
    decay = modes_of(rs)
    gain = modes_of(gg_ref)
    tap = [tp_ref[i * ROWS : (i + 1) * ROWS, :] for i in range(9)]
    unroll = 6

    def step(it, carry):
        state = list(carry)
        for o in range(unroll):
            t = it * unroll + 2 + o
            now, one, two = tok_rows(t), tok_rows(t - 1), tok_rows(t - 2)
            feat_k = tap[3] * ks[now, :] + tap[4] * ks[one, :] + tap[5] * ks[two, :]
            feat_v = tap[6] * vs[now, :] + tap[7] * vs[one, :] + tap[8] * vs[two, :]
            fq_ref[now, :] = tap[0] * qs[now, :] + tap[1] * qs[one, :] + tap[2] * qs[two, :]
            mixed = feat_k * feat_v
            state = [decay[m] * state[m] + gain[m] * mixed for m in range(MODES)]
            l_ref[now, :] = tree_sum(state)
        return tuple(state)

    zero = jnp.zeros((ROWS, LANES), f32)
    state = lax.fori_loop(0, (TOK - 2) // unroll, step, (zero,) * MODES)
    for m in range(MODES):
        f0_ref[m * ROWS : (m + 1) * ROWS, :] = state[m]


def edge_kernel(halo_ref, table_ref, f_ref, em_ref, hs):
    f0_ref = table_ref.at[T_STATE:T_RATE]
    rr_ref = table_ref.at[T_RATE:T_GAIN]
    gg_ref = table_ref.at[T_GAIN:T_TAP]
    tp_ref = table_ref.at[T_TAP:T_EDGE]
    edge_ref = table_ref.at[T_EDGE:T_END]
    halo = halo_ref[...].astype(f32)
    for i in range(3):
        for j in range(ROWS):
            hs[pl.ds(i * 8 * ROWS + j, 8, stride=ROWS), :] = halo[i * 8 : i * 8 + 8, lane_block(j)]

    def row(ref, i):
        return ref[i * ROWS : (i + 1) * ROWS, :]

    tap = [row(tp_ref, i) for i in range(9)]

    def feats(i, base):
        prev2, prev1 = row(hs, 8 * i + 6), row(hs, 8 * i + 7)
        tok0, tok1 = row(edge_ref, 2 * i), row(edge_ref, 2 * i + 1)
        w = tap[base : base + 3]
        return (
            w[0] * tok0 + w[1] * prev1 + w[2] * prev2,
            w[0] * tok1 + w[1] * tok0 + w[2] * prev1,
        )

    k0, k1 = feats(0, 3)
    v0, v1 = feats(1, 6)
    q0, q1 = feats(2, 0)
    m0, m1 = k0 * v0, k1 * v1
    for i, value in enumerate((m0, m1, q0, q1)):
        em_ref[i * ROWS : (i + 1) * ROWS, :] = value
    for i in range(MODES // 2):
        both = []
        for m in (2 * i, 2 * i + 1):
            rate, gain = row(rr_ref, m), row(gg_ref, m)
            both.append(
                row(f0_ref, m)
                + gain * (jnp.exp(rate * -127.0) * m0 + jnp.exp(rate * -126.0) * m1)
            )
        both = jnp.concatenate(both, axis=0).astype(bf16)
        for copy in range(NZ):
            f_ref[copy, i * 2 * ROWS : (i + 1) * 2 * ROWS, :] = both


def z_kernel(idx_ref, fz_ref, table_ref, u_ref, before_ref):
    z = idx_ref[1]
    d = jnp.exp(table_ref[T_RATE:T_GAIN, :] * -float(TOK * NQ))
    total = fz_ref[0].astype(f32)
    before = jnp.zeros_like(total)
    for i in range(1, NZ):
        before = jnp.where(z == i, total, before)
        total = d * total + fz_ref[i].astype(f32)
    total = total.astype(bf16)
    for i in range(NX):
        u_ref[i] = total
    before_ref[...] = before


def x_kernel(idx_ref, ux_ref, before_ref, f_ref, table_ref, y_ref):
    x, z, q = idx_ref[0], idx_ref[1], idx_ref[2]
    rate = table_ref[T_RATE:T_GAIN, :]
    d = jnp.exp(rate * -float(TOK * NQ * NZ))
    carry = jnp.zeros_like(rate)
    running = ux_ref[0].astype(f32)
    for i in range(1, NX):
        carry = jnp.where(x == i, running, carry)
        if i < NX - 1:
            running = d * running + ux_ref[i].astype(f32)
    before = before_ref[...] + jnp.exp(rate * (z * -(TOK * NQ)).astype(f32)) * carry
    after = jnp.exp(rate * -float(TOK * NQ)) * before + f_ref[0].astype(f32)
    before, after = before.astype(bf16), after.astype(bf16)
    for i in range(NQ):
        y_ref[i] = jnp.where(q < i, after, before)


def out_kernel(idx_ref, yq_ref, table_ref, em_ref, l_ref, fq_ref, out_ref, cs, ys):
    q = idx_ref[2]
    rate = table_ref[T_RATE:T_GAIN, :]
    own = tree_sum(
        [
            jnp.exp(rate * (((q + 3 - i) % NQ) * -TOK).astype(f32)) * yq_ref[i].astype(f32)
            for i in range(NQ)
        ]
    )
    decay_all = jnp.exp(-rate)
    gain_all = table_ref[T_GAIN:T_TAP, :]

    def tile(value, m):
        return value[m * ROWS : (m + 1) * ROWS, :]

    decay = [tile(decay_all, m) for m in range(MODES)]
    m0, m1, q0, q1 = [em_ref[i * ROWS : (i + 1) * ROWS, :] for i in range(4)]
    state = [decay[m] * tile(own, m) + tile(gain_all, m) * m0 for m in range(MODES)]
    ys[0:ROWS, :] = q0 * tree_sum(state)
    state = [decay[m] * state[m] + tile(gain_all, m) * m1 for m in range(MODES)]
    ys[ROWS : 2 * ROWS, :] = q1 * tree_sum(state)
    for m in range(MODES):
        cs[m * ROWS : (m + 1) * ROWS, :] = tile(decay_all, m)
    unroll = 6

    def step(it, carry_now):
        state = list(carry_now)
        for o in range(unroll):
            now = tok_rows(it * unroll + 2 + o)
            state = [cs[m * ROWS : (m + 1) * ROWS, :] * state[m] for m in range(MODES)]
            ys[now, :] = fq_ref[now, :] * (l_ref[now, :] + tree_sum(state))
        return tuple(state)

    lax.fori_loop(0, (TOK - 2) // unroll, step, tuple(state))
    for g in range(TOK // 16):
        for j in range(ROWS):
            halves = [
                ys[pl.ds((g * 16 + s * 8) * ROWS + j, 8, stride=ROWS), :] for s in range(2)
            ]
            out_ref[g * 16 : (g + 1) * 16, lane_block(j)] = jnp.concatenate(halves, axis=0).astype(bf16)


def weights_kernel(idx_ref, mask_ref, q_ref, k0_ref, k1_ref, k2_ref, swap_ref, k5_ref, w_ref, inv_ref):
    yarn_scale = 0.1 * math.log(yarn_factor) + 1.0
    coef = yarn_scale * yarn_scale / math.sqrt(HEAD_DIM) * math.log2(math.e)
    pieces = (k0_ref, k1_ref, k2_ref, swap_ref.at[0], swap_ref.at[1], k5_ref)
    odd = idx_ref[2] % 2 == 1
    shape = (TOK, TOK)
    causal = lax.broadcasted_iota(jnp.int32, shape, 1) <= lax.broadcasted_iota(jnp.int32, shape, 0)
    lane = lax.broadcasted_iota(jnp.int32, (TOK, LANES), 1)
    inverse = jnp.zeros((TOK, LANES), f32)
    for h in range(HEADS):
        query = q_ref[:, lane_block(h)]
        scores = []
        for i, piece in enumerate(pieces):
            s = lax.dot_general(
                query, piece[:, lane_block(h)], (((1,), (1,)), ((), ())), preferred_element_type=f32
            ) * coef
            allowed = mask_ref[0, jnp.where(odd, ODD_STEPS[i], EVEN_STEPS[i])] == 1
            visible = (causal & allowed) if i == 0 else jnp.broadcast_to(allowed, shape)
            scores.append(jnp.where(visible, s, -1e30))
        top = scores[0]
        for s in scores[1:]:
            top = jnp.maximum(top, s)
        top = jnp.max(top, axis=1, keepdims=True)
        total = None
        for i, s in enumerate(scores):
            w = jnp.exp2(s - top)
            total = w if total is None else total + w
            w_ref[h, :, lane_block(i)] = w.astype(bf16)
        total = jnp.sum(total, axis=1, keepdims=True)
        inverse = jnp.where(lane == h, 1.0 / total, inverse)
    inv_ref[...] = inverse


def attend_kernel(w_ref, inv_ref, v0_ref, v1_ref, v2_ref, swap_ref, v5_ref, a_ref, sq_ref):
    pieces = (v0_ref, v1_ref, v2_ref, swap_ref.at[0], swap_ref.at[1], v5_ref)
    inverse = inv_ref[...]
    squares = None
    for h in range(HEADS):
        acc = None
        for i, piece in enumerate(pieces):
            part = jnp.dot(w_ref[h, :, lane_block(i)], piece[:, lane_block(h)], preferred_element_type=f32)
            acc = part if acc is None else acc + part
        acc = acc * inverse[:, h : h + 1]
        a_ref[:, lane_block(h)] = acc
        squares = acc * acc if squares is None else squares + acc * acc
    sums = jnp.sum(squares, axis=1, keepdims=True)
    shape = (TOK, TOK)
    diag = lax.broadcasted_iota(jnp.int32, shape, 1) == lax.broadcasted_iota(jnp.int32, shape, 0)
    sq_ref[...] = jnp.sum(jnp.where(diag, sums, 0.0), axis=0, keepdims=True)


def norm_kernel(a_ref, sq_ref, gain_ref, out_ref):
    shape = (TOK, TOK)
    diag = lax.broadcasted_iota(jnp.int32, shape, 1) == lax.broadcasted_iota(jnp.int32, shape, 0)
    sums = jnp.sum(jnp.where(diag, sq_ref[...], 0.0), axis=1, keepdims=True)
    scale = lax.rsqrt(sums / float(WIDTH * 4) + norm_eps)
    out_ref[...] = (a_ref[...] * scale * gain_ref[...]).astype(bf16)


def quad_groups():
    return [[g * NQ + q for q in range(NQ)] for g in range(NX * NZ)]


def z_groups():
    return [[(x * NZ + z) * NQ + q for z in range(NZ)] for x in range(NX) for q in range(NQ)]


def x_groups():
    return [[(x * NZ + z) * NQ + q for x in range(NX)] for z in range(NZ) for q in range(NQ)]


def ahead(value, steps):
    return lax.ppermute(value, "ctx", [(i, (i + steps) % N_CTX) for i in range(N_CTX)])


def core_swap(value):
    return lax.ppermute(value, "ctx", [(i, i ^ 1) for i in range(N_CTX)])


def ahead_extra(value):
    return lax.ppermute(
        value, "ctx", [(i, (i + (5 if i % 2 else 1)) % N_CTX) for i in range(N_CTX)]
    )


def window_far(value):
    return ahead(value, 2), ahead(value, 4), ahead_extra(value)


def pair_of(a, b):
    return call(pair_kernel, sds((2, TOK, WIDTH), bf16), (a, b))


def local(
    hyena_q, hyena_k, hyena_v, short_taps, residues, rates, queries, keys, offsets, block_mask, out_gain
):
    me = lax.axis_index("ctx")
    idx = jnp.stack([me // (NZ * NQ), (me // NQ) % NZ, me % NQ]).astype(jnp.int32)
    dma = pltpu.SemaphoreType.DMA
    hyena = jnp.concatenate([hyena_k, hyena_v, hyena_q], axis=0)
    rim = jnp.concatenate([hyena[(i + 1) * TOK - 8 : (i + 1) * TOK] for i in range(3)], axis=0)
    halo = lax.ppermute(rim, "ctx", [(i, i + 1) for i in range(N_CTX - 1)])

    angles = (offsets[me] + jnp.arange(TOK, dtype=jnp.int32)).astype(f32)[:, None] * head_freqs(HEAD_DIM)[None, :]
    cosine, sine = jnp.cos(angles), jnp.sin(angles)
    q_rot, k_rot = call(
        rotate_kernel,
        [sds((TOK, WIDTH), bf16)] * 2,
        (
            queries,
            keys,
            jnp.concatenate([cosine, cosine], axis=1),
            jnp.concatenate([-sine, sine], axis=1),
        ),
        scratch=[pltpu.VMEM((TOK, WIDTH), bf16)] * 2 + [dma((2,))],
        hbm=(0, 1),
    )

    big, small = sds((TOK * ROWS, LANES), f32), sds((MODES * ROWS, LANES), f32)
    params = jnp.concatenate([rates, residues, short_taps.reshape(9, WIDTH)], axis=0)
    l_rest, feat_q, table = call(
        local_kernel,
        [big, big, sds((T_END, LANES), f32)],
        (hyena, params),
        scratch=[pltpu.VMEM((TOK * ROWS, LANES), f32)] * 3 + [pltpu.VMEM((MODES * ROWS, LANES), f32)],
    )
    state, em = call(
        edge_kernel,
        [sds((NZ, MODES * ROWS, LANES), bf16), sds((4 * ROWS, LANES), f32)],
        (halo, table),
        scratch=[pltpu.VMEM((24 * ROWS, LANES), f32)],
    )
    along_z = lax.all_to_all(state, "ctx", 0, 0, tiled=True, axis_index_groups=z_groups())
    column, before = call(
        z_kernel, [sds((NX, MODES * ROWS, LANES), bf16), small], (idx, along_z, table), smem=(0,)
    )
    k_two = ahead(k_rot, 2)
    column, k_late = lax.optimization_barrier((column, k_rot))
    k_extra = ahead_extra(call(copy_kernel, sds((TOK, WIDTH), bf16), (k_late,), flops=5_000_000_000))
    along_x = lax.all_to_all(column, "ctx", 0, 0, tiled=True, axis_index_groups=x_groups())
    classes = call(
        x_kernel, sds((NQ, MODES * ROWS, LANES), bf16), (idx, along_x, before, state, table), smem=(0,)
    )
    classes, k_late = lax.optimization_barrier((classes, k_late))
    k_four = ahead(call(copy_kernel, sds((TOK, WIDTH), bf16), (k_late,), flops=5_000_000_000), 4)
    quad = lax.all_to_all(classes, "ctx", 0, 0, tiled=True, axis_index_groups=quad_groups())
    quad, k_extra, k_two = lax.optimization_barrier((quad, k_extra, k_two))
    hyena_out = call(
        out_kernel,
        sds((TOK, WIDTH), bf16),
        (idx, quad, table, em, l_rest, feat_q),
        scratch=[pltpu.VMEM((MODES * ROWS, LANES), f32), pltpu.VMEM((TOK * ROWS, LANES), f32)],
        smem=(0,),
    )
    v_two, v_four, v_extra = window_far(hyena_out)
    k_two, hyena_late = lax.optimization_barrier((k_two, hyena_out))
    k_swap = core_swap(pair_of(k_two, k_four))
    v_two, v_extra = lax.optimization_barrier((v_two, v_extra))
    v_swap = core_swap(pair_of(v_two, v_four))
    weights, inverse = call(
        weights_kernel,
        [sds((HEADS, TOK, 6 * TOK), bf16), sds((TOK, LANES), f32)],
        (idx, block_mask, q_rot, k_rot, k_two, k_four, k_swap, k_extra),
        smem=(0, 1),
    )
    attended, squares = call(
        attend_kernel,
        [sds((TOK, WIDTH), f32), sds((1, TOK), f32)],
        (weights, inverse, hyena_out, v_two, v_four, v_swap, v_extra),
    )
    total = lax.psum(squares, "ch")
    attn_out = call(norm_kernel, sds((TOK, WIDTH), bf16), (attended, total, out_gain[None, :]))
    return (hyena_out, attn_out)


def solution(mesh):
    return jax.shard_map(
        local,
        mesh=mesh,
        in_specs=(
            P("ctx", "ch"),
            P("ctx", "ch"),
            P("ctx", "ch"),
            P(None, None, "ch"),
            P(None, "ch"),
            P(None, "ch"),
            P("ctx", "ch"),
            P("ctx", "ch"),
            P(),
            P("ctx", None),
            P("ch"),
        ),
        out_specs=(P("ctx", "ch"), P("ctx", "ch")),
        check_vma=False,
    )
```

```python
import math

import jax
import jax.numpy as jnp
from jax import lax
from jax.experimental import pallas as pl
from jax.experimental.pallas import tpu as pltpu
from jax.sharding import PartitionSpec as P

HEAD_DIM = 128
MODES = 16
TOK = 128
WIDTH = 1024
HEADS = WIDTH // HEAD_DIM
LANES = 128
ROWS = WIDTH // LANES
NX, NZ, NQ = 4, 8, 4
N_CTX = NX * NZ * NQ
EVEN_STEPS = (0, 2, 4, 1, 3, 5)
ODD_STEPS = (0, 2, 4, 3, 5, 1)

orig_window = 8192.0
rope_base = 10000.0
yarn_factor = 128.0
norm_eps = 1e-05
f32 = jnp.float32
bf16 = jnp.bfloat16


def call(kernel, out_shape, args, scratch=(), smem=(), hbm=(), vmem=24, flops=1000000):
    specs = [
        pl.BlockSpec(
            memory_space=pltpu.SMEM if i in smem else pltpu.HBM if i in hbm else pltpu.VMEM
        )
        for i in range(len(args))
    ]
    single = not isinstance(out_shape, (list, tuple))
    outs = pl.BlockSpec(memory_space=pltpu.VMEM)
    return pl.pallas_call(
        kernel,
        out_shape=out_shape,
        in_specs=specs,
        out_specs=outs if single else [outs] * len(out_shape),
        scratch_shapes=list(scratch),
        compiler_params=pltpu.CompilerParams(vmem_limit_bytes=vmem * 1024 * 1024),
        cost_estimate=pl.CostEstimate(flops=flops, bytes_accessed=1000000, transcendentals=0),
    )(*args)


def sds(shape, dtype):
    return jax.ShapeDtypeStruct(shape, dtype)


def head_freqs(head_dim):
    half_dim = head_dim // 2
    base_freq = jnp.power(rope_base, -2.0 * jnp.arange(half_dim, dtype=f32) / head_dim)
    wave_ratio = orig_window * base_freq / (2.0 * math.pi)
    ramp_mix = jnp.clip((wave_ratio - 1.0) / 31.0, 0.0, 1.0)
    return base_freq * ramp_mix + base_freq / yarn_factor * (1.0 - ramp_mix)


def lane_block(j):
    return slice(j * LANES, (j + 1) * LANES)


def tok_rows(t):
    return pl.ds(pl.multiple_of(t * ROWS, ROWS), ROWS)


def tree_sum(items):
    items = list(items)
    while len(items) > 1:
        items = [
            items[i] + items[i + 1] if i + 1 < len(items) else items[i]
            for i in range(0, len(items), 2)
        ]
    return items[0]


def modes_of(ref):
    return [ref[m * ROWS : (m + 1) * ROWS, :] for m in range(MODES)]


def fetch(pairs, sems):
    copies = [
        pltpu.make_async_copy(src, dst, sems.at[i]) for i, (src, dst) in enumerate(pairs)
    ]
    for copy in copies:
        copy.start()
    return copies


def rim_kernel(k_hbm, v_hbm, q_hbm, out_ref, ks, vs, qs, sems):
    last = pl.ds(TOK - 16, 16)
    for copy in fetch(
        [(k_hbm.at[last, :], ks), (v_hbm.at[last, :], vs), (q_hbm.at[last, :], qs)], sems
    ):
        copy.wait()
    parts = []
    for src in (ks, vs, qs):
        parts.append(src[...].astype(f32)[8:16, :])
    parts.append(parts[0])
    out_ref[...] = jnp.concatenate(parts, axis=0).astype(bf16)


def rotate_kernel(q_hbm, k_hbm, cos_ref, sin_ref, qo_ref, ko_ref, q_ref, k_ref, sems):
    for copy in fetch([(q_hbm, q_ref), (k_hbm, k_ref)], sems):
        copy.wait()
    cosine = cos_ref[...]
    sine = sin_ref[...]
    for src, dst in ((k_ref, ko_ref), (q_ref, qo_ref)):
        for h in range(HEADS):
            x = src[:, lane_block(h)].astype(f32)
            dst[:, lane_block(h)] = (x * cosine + pltpu.roll(x, HEAD_DIM // 2, 1) * sine).astype(bf16)


T_STATE, T_RATE, T_GAIN, T_TAP, T_EDGE, T_END = 0, 128, 256, 384, 456, 504


def copy_kernel(src_ref, dst_ref):
    dst_ref[...] = src_ref[...]


def pair_kernel(a_ref, b_ref, out_ref):
    out_ref[0] = a_ref[...]
    out_ref[1] = b_ref[...]


def local_kernel(h_ref, p_ref, l_ref, fq_ref, table_ref, qs, ks, vs, rs):
    f0_ref = table_ref.at[T_STATE:T_RATE]
    rr_ref = table_ref.at[T_RATE:T_GAIN]
    gg_ref = table_ref.at[T_GAIN:T_TAP]
    tp_ref = table_ref.at[T_TAP:T_EDGE]
    edge_ref = table_ref.at[T_EDGE:T_END]
    for part in range(MODES // 8):
        for j in range(ROWS):
            rows = pl.ds(part * 8 * ROWS + j, 8, stride=ROWS)
            rr_ref[rows, :] = p_ref[part * 8 : part * 8 + 8, lane_block(j)]
            rs[rows, :] = p_ref[MODES + part * 8 : MODES + part * 8 + 8, lane_block(j)]
    for j in range(ROWS):
        tp_ref[pl.ds(j, 8, stride=ROWS), :] = p_ref[2 * MODES : 2 * MODES + 8, lane_block(j)]
        tp_ref[8 * ROWS + j : 8 * ROWS + j + 1, :] = p_ref[2 * MODES + 8 : 2 * MODES + 9, lane_block(j)]
    for i, dst in enumerate((ks, vs, qs)):
        for g in range(TOK // 16):
            block = h_ref[i * TOK + g * 16 : i * TOK + (g + 1) * 16, :].astype(f32)
            for s in range(2):
                for j in range(ROWS):
                    dst[pl.ds((g * 16 + s * 8) * ROWS + j, 8, stride=ROWS), :] = block[
                        s * 8 : s * 8 + 8, lane_block(j)
                    ]
    for i, src in enumerate((ks, vs, qs)):
        edge_ref[i * 2 * ROWS : (i + 1) * 2 * ROWS, :] = src[0 : 2 * ROWS, :]
    rate = rr_ref[...]
    x = 2.0 * rate
    series = x * (1.0 - x / 2.0 * (1.0 - x / 3.0 * (1.0 - x / 4.0 * (
        1.0 - x / 5.0 * (1.0 - x / 6.0 * (1.0 - x / 7.0))))))
    gg_ref[...] = rs[...] * jnp.sqrt(series)
    rs[...] = jnp.exp(-rate)
    decay = modes_of(rs)
    gain = modes_of(gg_ref)
    tap = [tp_ref[i * ROWS : (i + 1) * ROWS, :] for i in range(9)]
    unroll = 6

    def step(it, carry):
        state = list(carry)
        for o in range(unroll):
            t = it * unroll + 2 + o
            now, one, two = tok_rows(t), tok_rows(t - 1), tok_rows(t - 2)
            feat_k = tap[3] * ks[now, :] + tap[4] * ks[one, :] + tap[5] * ks[two, :]
            feat_v = tap[6] * vs[now, :] + tap[7] * vs[one, :] + tap[8] * vs[two, :]
            fq_ref[now, :] = tap[0] * qs[now, :] + tap[1] * qs[one, :] + tap[2] * qs[two, :]
            mixed = feat_k * feat_v
            state = [decay[m] * state[m] + gain[m] * mixed for m in range(MODES)]
            l_ref[now, :] = tree_sum(state)
        return tuple(state)

    zero = jnp.zeros((ROWS, LANES), f32)
    state = lax.fori_loop(0, (TOK - 2) // unroll, step, (zero,) * MODES)
    for m in range(MODES):
        f0_ref[m * ROWS : (m + 1) * ROWS, :] = state[m]


def edge_kernel(halo_ref, table_ref, f_ref, em_ref, hs):
    f0_ref = table_ref.at[T_STATE:T_RATE]
    rr_ref = table_ref.at[T_RATE:T_GAIN]
    gg_ref = table_ref.at[T_GAIN:T_TAP]
    tp_ref = table_ref.at[T_TAP:T_EDGE]
    edge_ref = table_ref.at[T_EDGE:T_END]
    halo = halo_ref[...].astype(f32)
    for i in range(3):
        for j in range(ROWS):
            hs[pl.ds(i * 8 * ROWS + j, 8, stride=ROWS), :] = halo[i * 8 : i * 8 + 8, lane_block(j)]

    def row(ref, i):
        return ref[i * ROWS : (i + 1) * ROWS, :]

    tap = [row(tp_ref, i) for i in range(9)]

    def feats(i, base):
        prev2, prev1 = row(hs, 8 * i + 6), row(hs, 8 * i + 7)
        tok0, tok1 = row(edge_ref, 2 * i), row(edge_ref, 2 * i + 1)
        w = tap[base : base + 3]
        return (
            w[0] * tok0 + w[1] * prev1 + w[2] * prev2,
            w[0] * tok1 + w[1] * tok0 + w[2] * prev1,
        )

    k0, k1 = feats(0, 3)
    v0, v1 = feats(1, 6)
    q0, q1 = feats(2, 0)
    m0, m1 = k0 * v0, k1 * v1
    for i, value in enumerate((m0, m1, q0, q1)):
        em_ref[i * ROWS : (i + 1) * ROWS, :] = value
    for i in range(MODES // 2):
        both = []
        for m in (2 * i, 2 * i + 1):
            rate, gain = row(rr_ref, m), row(gg_ref, m)
            both.append(
                row(f0_ref, m)
                + gain * (jnp.exp(rate * -127.0) * m0 + jnp.exp(rate * -126.0) * m1)
            )
        both = jnp.concatenate(both, axis=0).astype(bf16)
        for copy in range(NZ):
            f_ref[copy, i * 2 * ROWS : (i + 1) * 2 * ROWS, :] = both


def z_kernel(idx_ref, fz_ref, table_ref, u_ref, before_ref):
    z = idx_ref[1]
    d = jnp.exp(table_ref[T_RATE:T_GAIN, :] * -float(TOK * NQ))
    total = fz_ref[0].astype(f32)
    before = jnp.zeros_like(total)
    for i in range(1, NZ):
        before = jnp.where(z == i, total, before)
        total = d * total + fz_ref[i].astype(f32)
    total = total.astype(bf16)
    for i in range(NX):
        u_ref[i] = total
    before_ref[...] = before


def x_kernel(idx_ref, ux_ref, before_ref, f_ref, table_ref, y_ref):
    x, z, q = idx_ref[0], idx_ref[1], idx_ref[2]
    rate = table_ref[T_RATE:T_GAIN, :]
    d = jnp.exp(rate * -float(TOK * NQ * NZ))
    carry = jnp.zeros_like(rate)
    running = ux_ref[0].astype(f32)
    for i in range(1, NX):
        carry = jnp.where(x == i, running, carry)
        if i < NX - 1:
            running = d * running + ux_ref[i].astype(f32)
    before = before_ref[...] + jnp.exp(rate * (z * -(TOK * NQ)).astype(f32)) * carry
    after = jnp.exp(rate * -float(TOK * NQ)) * before + f_ref[0].astype(f32)
    before, after = before.astype(bf16), after.astype(bf16)
    for i in range(NQ):
        y_ref[i] = jnp.where(q < i, after, before)


def out_kernel(idx_ref, yq_ref, table_ref, em_ref, l_ref, fq_ref, out_ref, cs, ys):
    q = idx_ref[2]
    rate = table_ref[T_RATE:T_GAIN, :]
    own = tree_sum(
        [
            jnp.exp(rate * (((q + 3 - i) % NQ) * -TOK).astype(f32)) * yq_ref[i].astype(f32)
            for i in range(NQ)
        ]
    )
    decay_all = jnp.exp(-rate)
    gain_all = table_ref[T_GAIN:T_TAP, :]

    def tile(value, m):
        return value[m * ROWS : (m + 1) * ROWS, :]

    decay = [tile(decay_all, m) for m in range(MODES)]
    m0, m1, q0, q1 = [em_ref[i * ROWS : (i + 1) * ROWS, :] for i in range(4)]
    state = [decay[m] * tile(own, m) + tile(gain_all, m) * m0 for m in range(MODES)]
    ys[0:ROWS, :] = q0 * tree_sum(state)
    state = [decay[m] * state[m] + tile(gain_all, m) * m1 for m in range(MODES)]
    ys[ROWS : 2 * ROWS, :] = q1 * tree_sum(state)
    for m in range(MODES):
        cs[m * ROWS : (m + 1) * ROWS, :] = tile(decay_all, m)
    unroll = 6

    def step(it, carry_now):
        state = list(carry_now)
        for o in range(unroll):
            now = tok_rows(it * unroll + 2 + o)
            state = [cs[m * ROWS : (m + 1) * ROWS, :] * state[m] for m in range(MODES)]
            ys[now, :] = fq_ref[now, :] * (l_ref[now, :] + tree_sum(state))
        return tuple(state)

    lax.fori_loop(0, (TOK - 2) // unroll, step, tuple(state))
    for g in range(TOK // 16):
        for j in range(ROWS):
            halves = [
                ys[pl.ds((g * 16 + s * 8) * ROWS + j, 8, stride=ROWS), :] for s in range(2)
            ]
            out_ref[g * 16 : (g + 1) * 16, lane_block(j)] = jnp.concatenate(halves, axis=0).astype(bf16)


def weights_kernel(idx_ref, mask_ref, q_ref, k0_ref, k1_ref, k2_ref, swap_ref, k5_ref, w_ref, inv_ref):
    yarn_scale = 0.1 * math.log(yarn_factor) + 1.0
    coef = yarn_scale * yarn_scale / math.sqrt(HEAD_DIM) * math.log2(math.e)
    pieces = (k0_ref, k1_ref, k2_ref, swap_ref.at[0], swap_ref.at[1], k5_ref)
    odd = idx_ref[2] % 2 == 1
    shape = (TOK, TOK)
    causal = lax.broadcasted_iota(jnp.int32, shape, 1) <= lax.broadcasted_iota(jnp.int32, shape, 0)
    lane = lax.broadcasted_iota(jnp.int32, (TOK, LANES), 1)
    inverse = jnp.zeros((TOK, LANES), f32)
    for h in range(HEADS):
        query = q_ref[:, lane_block(h)]
        scores = []
        for i, piece in enumerate(pieces):
            s = lax.dot_general(
                query, piece[:, lane_block(h)], (((1,), (1,)), ((), ())), preferred_element_type=f32
            ) * coef
            allowed = mask_ref[0, jnp.where(odd, ODD_STEPS[i], EVEN_STEPS[i])] == 1
            visible = (causal & allowed) if i == 0 else jnp.broadcast_to(allowed, shape)
            scores.append(jnp.where(visible, s, -1e30))
        top = scores[0]
        for s in scores[1:]:
            top = jnp.maximum(top, s)
        top = jnp.max(top, axis=1, keepdims=True)
        total = None
        for i, s in enumerate(scores):
            w = jnp.exp2(s - top)
            total = w if total is None else total + w
            w_ref[h, :, lane_block(i)] = w.astype(bf16)
        total = jnp.sum(total, axis=1, keepdims=True)
        inverse = jnp.where(lane == h, 1.0 / total, inverse)
    inv_ref[...] = inverse


def attend_kernel(w_ref, inv_ref, v0_ref, v1_ref, v2_ref, swap_ref, v5_ref, a_ref, sq_ref):
    pieces = (v0_ref, v1_ref, v2_ref, swap_ref.at[0], swap_ref.at[1], v5_ref)
    inverse = inv_ref[...]
    squares = None
    for h in range(HEADS):
        acc = None
        for i, piece in enumerate(pieces):
            part = jnp.dot(w_ref[h, :, lane_block(i)], piece[:, lane_block(h)], preferred_element_type=f32)
            acc = part if acc is None else acc + part
        acc = acc * inverse[:, h : h + 1]
        a_ref[:, lane_block(h)] = acc
        squares = acc * acc if squares is None else squares + acc * acc
    sums = jnp.sum(squares, axis=1, keepdims=True)
    shape = (TOK, TOK)
    diag = lax.broadcasted_iota(jnp.int32, shape, 1) == lax.broadcasted_iota(jnp.int32, shape, 0)
    sq_ref[...] = jnp.sum(jnp.where(diag, sums, 0.0), axis=0, keepdims=True)


def norm_kernel(a_ref, sq_ref, gain_ref, out_ref):
    shape = (TOK, TOK)
    diag = lax.broadcasted_iota(jnp.int32, shape, 1) == lax.broadcasted_iota(jnp.int32, shape, 0)
    sums = jnp.sum(jnp.where(diag, sq_ref[...], 0.0), axis=1, keepdims=True)
    scale = lax.rsqrt(sums / float(WIDTH * 4) + norm_eps)
    out_ref[...] = (a_ref[...] * scale * gain_ref[...]).astype(bf16)


def quad_groups():
    return [[g * NQ + q for q in range(NQ)] for g in range(NX * NZ)]


def z_groups():
    return [[(x * NZ + z) * NQ + q for z in range(NZ)] for x in range(NX) for q in range(NQ)]


def x_groups():
    return [[(x * NZ + z) * NQ + q for x in range(NX)] for z in range(NZ) for q in range(NQ)]


def ahead(value, steps):
    return lax.ppermute(value, "ctx", [(i, (i + steps) % N_CTX) for i in range(N_CTX)])


def core_swap(value):
    return lax.ppermute(value, "ctx", [(i, i ^ 1) for i in range(N_CTX)])


def ahead_extra(value):
    return lax.ppermute(
        value, "ctx", [(i, (i + (5 if i % 2 else 1)) % N_CTX) for i in range(N_CTX)]
    )


def window_far(value):
    return ahead(value, 2), ahead(value, 4), ahead_extra(value)


def pair_of(a, b):
    return call(pair_kernel, sds((2, TOK, WIDTH), bf16), (a, b))


def local(
    hyena_q, hyena_k, hyena_v, short_taps, residues, rates, queries, keys, offsets, block_mask, out_gain
):
    me = lax.axis_index("ctx")
    idx = jnp.stack([me // (NZ * NQ), (me // NQ) % NZ, me % NQ]).astype(jnp.int32)
    dma = pltpu.SemaphoreType.DMA
    hyena = jnp.concatenate([hyena_k, hyena_v, hyena_q], axis=0)
    rim = call(
        rim_kernel,
        sds((32, WIDTH), bf16),
        (hyena_k, hyena_v, hyena_q),
        scratch=[pltpu.VMEM((16, WIDTH), bf16)] * 3 + [dma((3,))],
        hbm=(0, 1, 2),
        vmem=60,
    )
    halo = lax.ppermute(rim, "ctx", [(i, i + 1) for i in range(N_CTX - 1)])

    angles = (offsets[me] + jnp.arange(TOK, dtype=jnp.int32)).astype(f32)[:, None] * head_freqs(HEAD_DIM)[None, :]
    cosine, sine = jnp.cos(angles), jnp.sin(angles)
    q_rot, k_rot = call(
        rotate_kernel,
        [sds((TOK, WIDTH), bf16)] * 2,
        (
            queries,
            keys,
            jnp.concatenate([cosine, cosine], axis=1),
            jnp.concatenate([-sine, sine], axis=1),
        ),
        scratch=[pltpu.VMEM((TOK, WIDTH), bf16)] * 2 + [dma((2,))],
        hbm=(0, 1),
    )

    big, small = sds((TOK * ROWS, LANES), f32), sds((MODES * ROWS, LANES), f32)
    params = jnp.concatenate([rates, residues, short_taps.reshape(9, WIDTH)], axis=0)
    l_rest, feat_q, table = call(
        local_kernel,
        [big, big, sds((T_END, LANES), f32)],
        (hyena, params),
        scratch=[pltpu.VMEM((TOK * ROWS, LANES), f32)] * 3 + [pltpu.VMEM((MODES * ROWS, LANES), f32)],
    )
    state, em = call(
        edge_kernel,
        [sds((NZ, MODES * ROWS, LANES), bf16), sds((4 * ROWS, LANES), f32)],
        (halo, table),
        scratch=[pltpu.VMEM((24 * ROWS, LANES), f32)],
    )
    along_z = lax.all_to_all(state, "ctx", 0, 0, tiled=True, axis_index_groups=z_groups())
    column, before = call(
        z_kernel, [sds((NX, MODES * ROWS, LANES), bf16), small], (idx, along_z, table), smem=(0,)
    )
    k_two = ahead(k_rot, 2)
    column, k_late = lax.optimization_barrier((column, k_rot))
    k_extra = ahead_extra(call(copy_kernel, sds((TOK, WIDTH), bf16), (k_late,), flops=5_000_000_000))
    along_x = lax.all_to_all(column, "ctx", 0, 0, tiled=True, axis_index_groups=x_groups())
    classes = call(
        x_kernel, sds((NQ, MODES * ROWS, LANES), bf16), (idx, along_x, before, state, table), smem=(0,)
    )
    classes, k_late = lax.optimization_barrier((classes, k_late))
    k_four = ahead(call(copy_kernel, sds((TOK, WIDTH), bf16), (k_late,), flops=5_000_000_000), 4)
    quad = lax.all_to_all(classes, "ctx", 0, 0, tiled=True, axis_index_groups=quad_groups())
    quad, k_extra, k_two = lax.optimization_barrier((quad, k_extra, k_two))
    hyena_out = call(
        out_kernel,
        sds((TOK, WIDTH), bf16),
        (idx, quad, table, em, l_rest, feat_q),
        scratch=[pltpu.VMEM((MODES * ROWS, LANES), f32), pltpu.VMEM((TOK * ROWS, LANES), f32)],
        smem=(0,),
    )
    v_two, v_four, v_extra = window_far(hyena_out)
    k_two, hyena_late = lax.optimization_barrier((k_two, hyena_out))
    k_swap = core_swap(pair_of(k_two, k_four))
    v_two, v_extra = lax.optimization_barrier((v_two, v_extra))
    v_swap = core_swap(pair_of(v_two, v_four))
    weights, inverse = call(
        weights_kernel,
        [sds((HEADS, TOK, 6 * TOK), bf16), sds((TOK, LANES), f32)],
        (idx, block_mask, q_rot, k_rot, k_two, k_four, k_swap, k_extra),
        smem=(0, 1),
    )
    attended, squares = call(
        attend_kernel,
        [sds((TOK, WIDTH), f32), sds((1, TOK), f32)],
        (weights, inverse, hyena_out, v_two, v_four, v_swap, v_extra),
    )
    total = lax.psum(squares, "ch")
    attn_out = call(norm_kernel, sds((TOK, WIDTH), bf16), (attended, total, out_gain[None, :]))
    return (hyena_out, attn_out)


def solution(mesh):
    return jax.shard_map(
        local,
        mesh=mesh,
        in_specs=(
            P("ctx", "ch"),
            P("ctx", "ch"),
            P("ctx", "ch"),
            P(None, None, "ch"),
            P(None, "ch"),
            P(None, "ch"),
            P("ctx", "ch"),
            P("ctx", "ch"),
            P(),
            P("ctx", None),
            P("ch"),
        ),
        out_specs=(P("ctx", "ch"), P("ctx", "ch")),
        check_vma=False,
    )
```

```python
import math

import jax
import jax.numpy as jnp
from jax import lax
from jax.experimental import pallas as pl
from jax.experimental.pallas import tpu as pltpu
from jax.sharding import PartitionSpec as P

HEAD_DIM = 128
MODES = 16
TOK = 128
WIDTH = 1024
HEADS = WIDTH // HEAD_DIM
LANES = 128
ROWS = WIDTH // LANES
NX, NZ, NQ = 4, 8, 4
N_CTX = NX * NZ * NQ
EVEN_STEPS = (0, 2, 4, 1, 3, 5)
ODD_STEPS = (0, 2, 4, 3, 5, 1)

orig_window = 8192.0
rope_base = 10000.0
yarn_factor = 128.0
norm_eps = 1e-05
f32 = jnp.float32
bf16 = jnp.bfloat16


def call(kernel, out_shape, args, scratch=(), smem=(), hbm=(), vmem=24, flops=1000000):
    specs = [
        pl.BlockSpec(
            memory_space=pltpu.SMEM if i in smem else pltpu.HBM if i in hbm else pltpu.VMEM
        )
        for i in range(len(args))
    ]
    single = not isinstance(out_shape, (list, tuple))
    outs = pl.BlockSpec(memory_space=pltpu.VMEM)
    return pl.pallas_call(
        kernel,
        out_shape=out_shape,
        in_specs=specs,
        out_specs=outs if single else [outs] * len(out_shape),
        scratch_shapes=list(scratch),
        compiler_params=pltpu.CompilerParams(vmem_limit_bytes=vmem * 1024 * 1024),
        cost_estimate=pl.CostEstimate(flops=flops, bytes_accessed=1000000, transcendentals=0),
    )(*args)


def sds(shape, dtype):
    return jax.ShapeDtypeStruct(shape, dtype)


def head_freqs(head_dim):
    half_dim = head_dim // 2
    base_freq = jnp.power(rope_base, -2.0 * jnp.arange(half_dim, dtype=f32) / head_dim)
    wave_ratio = orig_window * base_freq / (2.0 * math.pi)
    ramp_mix = jnp.clip((wave_ratio - 1.0) / 31.0, 0.0, 1.0)
    return base_freq * ramp_mix + base_freq / yarn_factor * (1.0 - ramp_mix)


def lane_block(j):
    return slice(j * LANES, (j + 1) * LANES)


def tok_rows(t):
    return pl.ds(pl.multiple_of(t * ROWS, ROWS), ROWS)


def tree_sum(items):
    items = list(items)
    while len(items) > 1:
        items = [
            items[i] + items[i + 1] if i + 1 < len(items) else items[i]
            for i in range(0, len(items), 2)
        ]
    return items[0]


def modes_of(ref):
    return [ref[m * ROWS : (m + 1) * ROWS, :] for m in range(MODES)]


def fetch(pairs, sems):
    copies = [
        pltpu.make_async_copy(src, dst, sems.at[i]) for i, (src, dst) in enumerate(pairs)
    ]
    for copy in copies:
        copy.start()
    return copies


def rim_kernel(k_hbm, v_hbm, q_hbm, out_ref, ks, vs, qs, sems):
    last = pl.ds(TOK - 16, 16)
    for copy in fetch(
        [(k_hbm.at[last, :], ks), (v_hbm.at[last, :], vs), (q_hbm.at[last, :], qs)], sems
    ):
        copy.wait()
    parts = []
    for src in (ks, vs, qs):
        parts.append(src[...].astype(f32)[8:16, :])
    parts.append(parts[0])
    out_ref[...] = jnp.concatenate(parts, axis=0).astype(bf16)


def rotate_kernel(q_hbm, k_hbm, cos_ref, sin_ref, qo_ref, ko_ref, q_ref, k_ref, sems):
    for copy in fetch([(q_hbm, q_ref), (k_hbm, k_ref)], sems):
        copy.wait()
    cosine = cos_ref[...]
    sine = sin_ref[...]
    for src, dst in ((k_ref, ko_ref), (q_ref, qo_ref)):
        for h in range(HEADS):
            x = src[:, lane_block(h)].astype(f32)
            dst[:, lane_block(h)] = (x * cosine + pltpu.roll(x, HEAD_DIM // 2, 1) * sine).astype(bf16)


T_STATE, T_RATE, T_GAIN, T_TAP, T_EDGE, T_END = 0, 128, 256, 384, 456, 504


def copy_kernel(src_ref, dst_ref):
    dst_ref[...] = src_ref[...]


def pair_kernel(a_ref, b_ref, out_ref):
    out_ref[0] = a_ref[...]
    out_ref[1] = b_ref[...]


def local_kernel(h_ref, p_ref, l_ref, fq_ref, table_ref, qs, ks, vs, rs):
    f0_ref = table_ref.at[T_STATE:T_RATE]
    rr_ref = table_ref.at[T_RATE:T_GAIN]
    gg_ref = table_ref.at[T_GAIN:T_TAP]
    tp_ref = table_ref.at[T_TAP:T_EDGE]
    edge_ref = table_ref.at[T_EDGE:T_END]
    for part in range(MODES // 8):
        for j in range(ROWS):
            rows = pl.ds(part * 8 * ROWS + j, 8, stride=ROWS)
            rr_ref[rows, :] = p_ref[part * 8 : part * 8 + 8, lane_block(j)]
            rs[rows, :] = p_ref[MODES + part * 8 : MODES + part * 8 + 8, lane_block(j)]
    for j in range(ROWS):
        tp_ref[pl.ds(j, 8, stride=ROWS), :] = p_ref[2 * MODES : 2 * MODES + 8, lane_block(j)]
        tp_ref[8 * ROWS + j : 8 * ROWS + j + 1, :] = p_ref[2 * MODES + 8 : 2 * MODES + 9, lane_block(j)]
    for i, dst in enumerate((ks, vs, qs)):
        for g in range(TOK // 16):
            block = h_ref[i * TOK + g * 16 : i * TOK + (g + 1) * 16, :].astype(f32)
            for s in range(2):
                for j in range(ROWS):
                    dst[pl.ds((g * 16 + s * 8) * ROWS + j, 8, stride=ROWS), :] = block[
                        s * 8 : s * 8 + 8, lane_block(j)
                    ]
    for i, src in enumerate((ks, vs, qs)):
        edge_ref[i * 2 * ROWS : (i + 1) * 2 * ROWS, :] = src[0 : 2 * ROWS, :]
    rate = rr_ref[...]
    x = 2.0 * rate
    series = x * (1.0 - x / 2.0 * (1.0 - x / 3.0 * (1.0 - x / 4.0 * (
        1.0 - x / 5.0 * (1.0 - x / 6.0 * (1.0 - x / 7.0))))))
    gg_ref[...] = rs[...] * jnp.sqrt(series)
    rs[...] = jnp.exp(-rate)
    decay = modes_of(rs)
    gain = modes_of(gg_ref)
    tap = [tp_ref[i * ROWS : (i + 1) * ROWS, :] for i in range(9)]
    unroll = 6

    def step(it, carry):
        state = list(carry)
        for o in range(unroll):
            t = it * unroll + 2 + o
            now, one, two = tok_rows(t), tok_rows(t - 1), tok_rows(t - 2)
            feat_k = tap[3] * ks[now, :] + tap[4] * ks[one, :] + tap[5] * ks[two, :]
            feat_v = tap[6] * vs[now, :] + tap[7] * vs[one, :] + tap[8] * vs[two, :]
            fq_ref[now, :] = tap[0] * qs[now, :] + tap[1] * qs[one, :] + tap[2] * qs[two, :]
            mixed = feat_k * feat_v
            state = [decay[m] * state[m] + gain[m] * mixed for m in range(MODES)]
            l_ref[now, :] = tree_sum(state)
        return tuple(state)

    zero = jnp.zeros((ROWS, LANES), f32)
    state = lax.fori_loop(0, (TOK - 2) // unroll, step, (zero,) * MODES)
    for m in range(MODES):
        f0_ref[m * ROWS : (m + 1) * ROWS, :] = state[m]


def edge_kernel(halo_ref, table_ref, f_ref, em_ref, own_ref, hs):
    f0_ref = table_ref.at[T_STATE:T_RATE]
    rr_ref = table_ref.at[T_RATE:T_GAIN]
    gg_ref = table_ref.at[T_GAIN:T_TAP]
    tp_ref = table_ref.at[T_TAP:T_EDGE]
    edge_ref = table_ref.at[T_EDGE:T_END]
    halo = halo_ref[...].astype(f32)
    for i in range(3):
        for j in range(ROWS):
            hs[pl.ds(i * 8 * ROWS + j, 8, stride=ROWS), :] = halo[i * 8 : i * 8 + 8, lane_block(j)]

    def row(ref, i):
        return ref[i * ROWS : (i + 1) * ROWS, :]

    tap = [row(tp_ref, i) for i in range(9)]

    def feats(i, base):
        prev2, prev1 = row(hs, 8 * i + 6), row(hs, 8 * i + 7)
        tok0, tok1 = row(edge_ref, 2 * i), row(edge_ref, 2 * i + 1)
        w = tap[base : base + 3]
        return (
            w[0] * tok0 + w[1] * prev1 + w[2] * prev2,
            w[0] * tok1 + w[1] * tok0 + w[2] * prev1,
        )

    k0, k1 = feats(0, 3)
    v0, v1 = feats(1, 6)
    q0, q1 = feats(2, 0)
    m0, m1 = k0 * v0, k1 * v1
    for i, value in enumerate((m0, m1, q0, q1)):
        em_ref[i * ROWS : (i + 1) * ROWS, :] = value
    for i in range(MODES // 2):
        both = []
        for m in (2 * i, 2 * i + 1):
            rate, gain = row(rr_ref, m), row(gg_ref, m)
            both.append(
                row(f0_ref, m)
                + gain * (jnp.exp(rate * -127.0) * m0 + jnp.exp(rate * -126.0) * m1)
            )
        both = jnp.concatenate(both, axis=0).astype(bf16)
        own_ref[i * 2 * ROWS : (i + 1) * 2 * ROWS, :] = both
        for copy in range(NZ):
            f_ref[copy, i * 2 * ROWS : (i + 1) * 2 * ROWS, :] = both


def z_kernel(idx_ref, fz_ref, table_ref, u_ref, before_ref):
    z = idx_ref[1]
    d = jnp.exp(table_ref[T_RATE:T_GAIN, :] * -float(TOK * NQ))
    total = fz_ref[0].astype(f32)
    before = jnp.zeros_like(total)
    for i in range(1, NZ):
        before = jnp.where(z == i, total, before)
        total = d * total + fz_ref[i].astype(f32)
    total = total.astype(bf16)
    for i in range(NX):
        u_ref[i] = total
    before_ref[...] = before


def x_kernel(idx_ref, ux_ref, before_ref, f_ref, table_ref, y_ref):
    x, z, q = idx_ref[0], idx_ref[1], idx_ref[2]
    rate = table_ref[T_RATE:T_GAIN, :]
    d = jnp.exp(rate * -float(TOK * NQ * NZ))
    carry = jnp.zeros_like(rate)
    running = ux_ref[0].astype(f32)
    for i in range(1, NX):
        carry = jnp.where(x == i, running, carry)
        if i < NX - 1:
            running = d * running + ux_ref[i].astype(f32)
    before = before_ref[...] + jnp.exp(rate * (z * -(TOK * NQ)).astype(f32)) * carry
    after = jnp.exp(rate * -float(TOK * NQ)) * before + f_ref[...].astype(f32)
    before, after = before.astype(bf16), after.astype(bf16)
    for i in range(NQ):
        y_ref[i] = jnp.where(q < i, after, before)


def out_kernel(idx_ref, yq_ref, table_ref, em_ref, l_ref, fq_ref, out_ref, ys):
    q = idx_ref[2]
    rate = table_ref[T_RATE:T_GAIN, :]
    own = tree_sum(
        [
            jnp.exp(rate * (((q + 3 - i) % NQ) * -TOK).astype(f32)) * yq_ref[i].astype(f32)
            for i in range(NQ)
        ]
    )
    decay_all = jnp.exp(-rate)
    gain_all = table_ref[T_GAIN:T_TAP, :]

    def tile(value, m):
        return value[m * ROWS : (m + 1) * ROWS, :]

    decay = [tile(decay_all, m) for m in range(MODES)]
    m0, m1, q0, q1 = [em_ref[i * ROWS : (i + 1) * ROWS, :] for i in range(4)]
    state = [decay[m] * tile(own, m) + tile(gain_all, m) * m0 for m in range(MODES)]
    ys[0:ROWS, :] = q0 * tree_sum(state)
    state = [decay[m] * state[m] + tile(gain_all, m) * m1 for m in range(MODES)]
    ys[ROWS : 2 * ROWS, :] = q1 * tree_sum(state)
    unroll = 18

    def step(it, carry_now):
        state = list(carry_now)
        for o in range(unroll):
            now = tok_rows(it * unroll + 2 + o)
            state = [decay[m] * state[m] for m in range(MODES)]
            ys[now, :] = fq_ref[now, :] * (l_ref[now, :] + tree_sum(state))
        return tuple(state)

    lax.fori_loop(0, (TOK - 2) // unroll, step, tuple(state))
    for g in range(TOK // 16):
        for j in range(ROWS):
            halves = [
                ys[pl.ds((g * 16 + s * 8) * ROWS + j, 8, stride=ROWS), :] for s in range(2)
            ]
            out_ref[g * 16 : (g + 1) * 16, lane_block(j)] = jnp.concatenate(halves, axis=0).astype(bf16)


def weights_kernel(idx_ref, mask_ref, q_ref, k0_ref, k1_ref, k2_ref, swap_ref, k5_ref, w_ref, inv_ref):
    yarn_scale = 0.1 * math.log(yarn_factor) + 1.0
    coef = yarn_scale * yarn_scale / math.sqrt(HEAD_DIM) * math.log2(math.e)
    pieces = (k0_ref, k1_ref, k2_ref, swap_ref.at[0], swap_ref.at[1], k5_ref)
    odd = idx_ref[2] % 2 == 1
    shape = (TOK, TOK)
    causal = lax.broadcasted_iota(jnp.int32, shape, 1) <= lax.broadcasted_iota(jnp.int32, shape, 0)
    lane = lax.broadcasted_iota(jnp.int32, (TOK, LANES), 1)
    inverse = jnp.zeros((TOK, LANES), f32)
    for h in range(HEADS):
        query = q_ref[:, lane_block(h)]
        scores = []
        for i, piece in enumerate(pieces):
            s = lax.dot_general(
                query, piece[:, lane_block(h)], (((1,), (1,)), ((), ())), preferred_element_type=f32
            ) * coef
            allowed = mask_ref[0, jnp.where(odd, ODD_STEPS[i], EVEN_STEPS[i])] == 1
            visible = (causal & allowed) if i == 0 else jnp.broadcast_to(allowed, shape)
            scores.append(jnp.where(visible, s, -1e30))
        top = scores[0]
        for s in scores[1:]:
            top = jnp.maximum(top, s)
        top = jnp.max(top, axis=1, keepdims=True)
        total = None
        for i, s in enumerate(scores):
            w = jnp.exp2(s - top)
            total = w if total is None else total + w
            w_ref[h, :, lane_block(i)] = w.astype(bf16)
        total = jnp.sum(total, axis=1, keepdims=True)
        inverse = jnp.where(lane == h, 1.0 / total, inverse)
    inv_ref[...] = inverse


def attend_kernel(w_ref, inv_ref, v0_ref, v1_ref, v2_ref, swap_ref, v5_ref, a_ref, sq_ref):
    pieces = (v0_ref, v1_ref, v2_ref, swap_ref.at[0], swap_ref.at[1], v5_ref)
    inverse = inv_ref[...]
    squares = None
    for h in range(HEADS):
        acc = None
        for i, piece in enumerate(pieces):
            part = jnp.dot(w_ref[h, :, lane_block(i)], piece[:, lane_block(h)], preferred_element_type=f32)
            acc = part if acc is None else acc + part
        acc = acc * inverse[:, h : h + 1]
        a_ref[:, lane_block(h)] = acc
        squares = acc * acc if squares is None else squares + acc * acc
    sums = jnp.sum(squares, axis=1, keepdims=True)
    shape = (TOK, TOK)
    diag = lax.broadcasted_iota(jnp.int32, shape, 1) == lax.broadcasted_iota(jnp.int32, shape, 0)
    sq_ref[...] = jnp.sum(jnp.where(diag, sums, 0.0), axis=0, keepdims=True)


def norm_kernel(a_ref, sq_ref, gain_ref, out_ref):
    shape = (TOK, TOK)
    diag = lax.broadcasted_iota(jnp.int32, shape, 1) == lax.broadcasted_iota(jnp.int32, shape, 0)
    sums = jnp.sum(jnp.where(diag, sq_ref[...], 0.0), axis=1, keepdims=True)
    scale = lax.rsqrt(sums / float(WIDTH * 4) + norm_eps)
    out_ref[...] = (a_ref[...] * scale * gain_ref[...]).astype(bf16)


def quad_groups():
    return [[g * NQ + q for q in range(NQ)] for g in range(NX * NZ)]


def z_groups():
    return [[(x * NZ + z) * NQ + q for z in range(NZ)] for x in range(NX) for q in range(NQ)]


def x_groups():
    return [[(x * NZ + z) * NQ + q for x in range(NX)] for z in range(NZ) for q in range(NQ)]


def ahead(value, steps):
    return lax.ppermute(value, "ctx", [(i, (i + steps) % N_CTX) for i in range(N_CTX)])


def core_swap(value):
    return lax.ppermute(value, "ctx", [(i, i ^ 1) for i in range(N_CTX)])


def ahead_extra(value):
    return lax.ppermute(
        value, "ctx", [(i, (i + (5 if i % 2 else 1)) % N_CTX) for i in range(N_CTX)]
    )


def window_far(value):
    return ahead(value, 2), ahead(value, 4), ahead_extra(value)


def pair_of(a, b):
    return call(pair_kernel, sds((2, TOK, WIDTH), bf16), (a, b))


def local(
    hyena_q, hyena_k, hyena_v, short_taps, residues, rates, queries, keys, offsets, block_mask, out_gain
):
    me = lax.axis_index("ctx")
    idx = jnp.stack([me // (NZ * NQ), (me // NQ) % NZ, me % NQ]).astype(jnp.int32)
    dma = pltpu.SemaphoreType.DMA
    hyena = jnp.concatenate([hyena_k, hyena_v, hyena_q], axis=0)
    rim = call(
        rim_kernel,
        sds((32, WIDTH), bf16),
        (hyena_k, hyena_v, hyena_q),
        scratch=[pltpu.VMEM((16, WIDTH), bf16)] * 3 + [dma((3,))],
        hbm=(0, 1, 2),
        vmem=60,
    )
    halo = lax.ppermute(rim, "ctx", [(i, i + 1) for i in range(N_CTX - 1)])

    angles = (offsets[me] + jnp.arange(TOK, dtype=jnp.int32)).astype(f32)[:, None] * head_freqs(HEAD_DIM)[None, :]
    cosine, sine = jnp.cos(angles), jnp.sin(angles)
    q_rot, k_rot = call(
        rotate_kernel,
        [sds((TOK, WIDTH), bf16)] * 2,
        (
            queries,
            keys,
            jnp.concatenate([cosine, cosine], axis=1),
            jnp.concatenate([-sine, sine], axis=1),
        ),
        scratch=[pltpu.VMEM((TOK, WIDTH), bf16)] * 2 + [dma((2,))],
        hbm=(0, 1),
    )

    big, small = sds((TOK * ROWS, LANES), f32), sds((MODES * ROWS, LANES), f32)
    params = jnp.concatenate([rates, residues, short_taps.reshape(9, WIDTH)], axis=0)
    l_rest, feat_q, table = call(
        local_kernel,
        [big, big, sds((T_END, LANES), f32)],
        (hyena, params),
        scratch=[pltpu.VMEM((TOK * ROWS, LANES), f32)] * 3 + [pltpu.VMEM((MODES * ROWS, LANES), f32)],
    )
    state, em, own_state = call(
        edge_kernel,
        [
            sds((NZ, MODES * ROWS, LANES), bf16),
            sds((4 * ROWS, LANES), f32),
            sds((MODES * ROWS, LANES), bf16),
        ],
        (halo, table),
        scratch=[pltpu.VMEM((24 * ROWS, LANES), f32)],
    )
    along_z = lax.all_to_all(state, "ctx", 0, 0, tiled=True, axis_index_groups=z_groups())
    column, before = call(
        z_kernel, [sds((NX, MODES * ROWS, LANES), bf16), small], (idx, along_z, table), smem=(0,)
    )
    k_two = ahead(k_rot, 2)
    column, k_late = lax.optimization_barrier((column, k_rot))
    k_extra = ahead_extra(call(copy_kernel, sds((TOK, WIDTH), bf16), (k_late,), flops=5_000_000_000))
    along_x = lax.all_to_all(column, "ctx", 0, 0, tiled=True, axis_index_groups=x_groups())
    classes = call(
        x_kernel, sds((NQ, MODES * ROWS, LANES), bf16), (idx, along_x, before, own_state, table), smem=(0,)
    )
    classes, k_late = lax.optimization_barrier((classes, k_late))
    k_four = ahead(call(copy_kernel, sds((TOK, WIDTH), bf16), (k_late,), flops=5_000_000_000), 4)
    quad = lax.all_to_all(classes, "ctx", 0, 0, tiled=True, axis_index_groups=quad_groups())
    quad, k_extra, k_two = lax.optimization_barrier((quad, k_extra, k_two))
    hyena_out = call(
        out_kernel,
        sds((TOK, WIDTH), bf16),
        (idx, quad, table, em, l_rest, feat_q),
        scratch=[pltpu.VMEM((TOK * ROWS, LANES), f32)],
        smem=(0,),
    )
    v_two, v_four, v_extra = window_far(hyena_out)
    k_two, hyena_late = lax.optimization_barrier((k_two, hyena_out))
    k_swap = core_swap(pair_of(k_two, k_four))
    v_two, v_extra = lax.optimization_barrier((v_two, v_extra))
    v_swap = core_swap(pair_of(v_two, v_four))
    weights, inverse = call(
        weights_kernel,
        [sds((HEADS, TOK, 6 * TOK), bf16), sds((TOK, LANES), f32)],
        (idx, block_mask, q_rot, k_rot, k_two, k_four, k_swap, k_extra),
        smem=(0, 1),
    )
    attended, squares = call(
        attend_kernel,
        [sds((TOK, WIDTH), f32), sds((1, TOK), f32)],
        (weights, inverse, hyena_out, v_two, v_four, v_swap, v_extra),
    )
    total = lax.psum(squares, "ch")
    attn_out = call(norm_kernel, sds((TOK, WIDTH), bf16), (attended, total, out_gain[None, :]))
    return (hyena_out, attn_out)


def solution(mesh):
    return jax.shard_map(
        local,
        mesh=mesh,
        in_specs=(
            P("ctx", "ch"),
            P("ctx", "ch"),
            P("ctx", "ch"),
            P(None, None, "ch"),
            P(None, "ch"),
            P(None, "ch"),
            P("ctx", "ch"),
            P("ctx", "ch"),
            P(),
            P("ctx", None),
            P("ch"),
        ),
        out_specs=(P("ctx", "ch"), P("ctx", "ch")),
        check_vma=False,
    )
```
